32 devices in a mesh: expert: 8 (over y, x, core), dp: 4 (over z).
Axes of the slice: x: 2, y: 2, z: 4, core: 2. Of those that a mesh axis runs over, the one named last changes fastest.
Arguments:
- tokens: bfloat16 [2048, 2048], P('expert'), may hold values from -6 to 6
- grad_out: bfloat16 [2048, 2048], P('expert'), may hold values from -6 to 6
- expert_ids: int32 [2048, 2], P('expert'), may hold values from 0 to 7, all different within a row; in each aligned block of 256 rows (0 to 255, 256 to 511, ...) at most 96 rows name the same one
- gate_vals: float32 [2048, 2], P('expert'), may hold values from 0.2 to 1
- w_gate: bfloat16 [8, 2048, 4096], P('expert', None, 'dp'), may hold values from -0.125 to 0.125
- w_up: bfloat16 [8, 2048, 4096], P('expert', None, 'dp'), may hold values from -0.125 to 0.125
- w_down: bfloat16 [8, 4096, 2048], P('expert', 'dp'), may hold values from -0.09375 to 0.09375
Outputs:
- grad_tokens: bfloat16 [2048, 2048], P('expert', 'dp')
- grad_gate: bfloat16 [8, 2048, 4096], P('expert', None, 'dp')
- grad_up: bfloat16 [8, 2048, 4096], P('expert', None, 'dp')
- grad_down: bfloat16 [8, 4096, 2048], P('expert', 'dp')
The draws below stay inside these ranges and needn't reach their ends.
Inputs may be any that keep to these rules, and one draw needn't show every extreme that they name: `expert_ids`: each row names 2 different experts; among the 256 rows of one index of the expert axis no expert is named more than 96 times.
All inputs are finite; a program needn't handle non-finite values.
Results may differ from the reference program's by a relative error of at most 0.0058.
Values may be sent and summed in bfloat16 or wider, within the bound.
No kernel may reach another device: no remote copies, remote signals or barrier semaphores. Data moves between devices by JAX's collectives and lax.ppermute only.
A program may use at most 128 MiB of HBM per device.

```python
import math
import jax
import jax.numpy as jnp
import numpy as np
from jax import lax

D = 2048
FF = 4096
TOP = 2
TOK_DEV = 256
EXPERTS = 8
CAP = 96
TOKENS = 2048
N_EXPERT = 8


def block_scale(own_key, shape, pieces, low, top_value):
    factor_of, own = 1.0, jax.random.fold_in(own_key, 6)
    for dim, blocks in pieces:
        steps = jnp.exp(jax.random.uniform(jax.random.fold_in(own, dim), (blocks,), jnp.float32, low / len(pieces), top_value / len(pieces)))
        factor_of = factor_of * jnp.repeat(steps, shape[dim] // blocks).reshape([-1 if axis == dim else 1 for axis in range(len(shape))])
    return factor_of


def assign_block(rng, own, number, rows, amount, top, reach, lean):
    order = jax.random.permutation(rng, amount)
    heavy_load, usual = load_shares(amount, rows * top, reach, lean, True), load_shares(amount, rows * top, reach, lean, False)
    places = jnp.arange(amount)

    def named(lengths, turn):
        used = int((lengths > 0).sum())
        fixed = max(1, used // 4)
        shifted = fixed + (places - fixed + turn * (used - fixed)) % max(1, amount - fixed)
        return jnp.zeros((amount,), jnp.int32).at[order[jnp.where(places < fixed, places, shifted)]].set(jnp.asarray(lengths, jnp.int32))

    lengths = jnp.where(number % 4 == 0, named(heavy_load, number // 4), named(usual, number - number // 4 - 1))
    mixed = jax.random.permutation(jax.random.fold_in(own, 3), amount)
    donor, taker = mixed[0:amount // 2 * 2:2], mixed[1:amount // 2 * 2:2]
    slack = jnp.minimum(lengths[donor] - 1, reach - lengths[taker]) // 2
    slack = jnp.where((donor == order[0]) | (taker == order[0]) | (lengths[taker] == 0), 0, jnp.maximum(slack, 0))
    shifted = jax.random.randint(jax.random.fold_in(own, 4), (amount // 2,), 0, 1 << 20) % (slack + 1)
    lengths = lengths.at[donor].add(-shifted).at[taker].add(shifted)
    members = jnp.searchsorted(jnp.cumsum(lengths), jnp.arange(rows * top), side="right").astype(jnp.int32)
    listing = members.reshape(top, rows).T
    listing = listing[jax.random.permutation(jax.random.fold_in(own, 1), rows)]
    turn = jax.random.randint(jax.random.fold_in(own, 2), (rows, 1), 0, top)
    return jnp.take_along_axis(listing, (jnp.arange(top)[None, :] + turn) % top, axis=1)


def load_shares(amount, total, most, lean, full):
    portions = [(1 << 20) // math.isqrt(grade ** lean) + 1 for grade in range(1, amount + 1)]
    largest = most if full else min(most, max(-(-total // amount), total * portions[0] // sum(portions)))
    least = 1 if total - largest >= amount - 1 else 0
    holding, surplus = [largest] + [least] * (amount - 1), total - largest - least * (amount - 1)
    while surplus > 0:
        free = [i for i in range(1, amount) if holding[i] < largest] or [i for i in range(1, amount) if holding[i] < most]
        pool, left = sum([portions[i] for i in free]), surplus
        for i in free:
            extra = min(most - holding[i], max(1, left * portions[i] // pool), surplus)
            holding[i] = holding[i] + extra
            surplus = surplus - extra
    return np.array(holding)


def centred(rng, shape, deviation, limit, split=(), kind=jnp.bfloat16):
    factor_of = block_scale(rng, shape, split, -0.22, 0.18) if split else 1.0
    values = jax.random.normal(rng, shape, jnp.float32) * deviation * factor_of
    return jnp.minimum(jnp.maximum(values, -limit), limit).astype(kind)


def setup_inputs(seed: int = 0) -> dict:
    splits = jax.random.split(jax.random.key(seed), 8)
    tokens = centred(splits[0], (TOKENS, D), 1.0, 6.0, ((0, 8),))
    grad_out = centred(splits[1], (TOKENS, D), 1.0, 6.0, ((0, 8),))
    expert_ids_keys = jax.random.split(jax.random.fold_in(splits[2], 1), TOKENS // TOK_DEV)
    expert_ids_turns = jax.random.permutation(jax.random.fold_in(splits[2], 3), TOKENS // TOK_DEV)
    expert_ids = jax.vmap(lambda own, number: assign_block(jax.random.fold_in(splits[2], 2), own, number, TOK_DEV, EXPERTS, TOP, CAP, 1))(expert_ids_keys, expert_ids_turns).reshape((TOKENS, TOP))
    gate_vals = jnp.clip(0.2 + 0.8 * jax.random.uniform(splits[3], (TOKENS, TOP), jnp.float32) ** block_scale(splits[3], (TOKENS, TOP), ((0, 8),), -0.2, 0.2), 0.2, 1.0)
    w_gate = centred(splits[4], (EXPERTS, D, FF), D ** -0.5, 0.125, ((0, 8), (2, 4)))
    w_up = centred(splits[5], (EXPERTS, D, FF), D ** -0.5, 0.125, ((0, 8), (2, 4)))
    w_down = centred(splits[6], (EXPERTS, FF, D), FF ** -0.5, 0.09375, ((0, 8), (1, 4)))
    return {"tokens": tokens, "grad_out": grad_out, "expert_ids": expert_ids, "gate_vals": gate_vals, "w_gate": w_gate, "w_up": w_up, "w_down": w_down}


def reference(tokens, grad_out, expert_ids, gate_vals, w_gate, w_up, w_down):
    most = N_EXPERT * CAP
    grad_f = grad_out.astype(jnp.float32)

    def one_expert(grad_acc, index):
        match = expert_ids == index
        gate_row = jnp.sum(jnp.where(match, gate_vals, jnp.zeros_like(gate_vals)), axis=1)
        picked = jnp.any(match, axis=1)
        order = jnp.argsort(jnp.where(picked, 0, 1).astype(jnp.int32), stable=True)[:most].astype(jnp.int32)
        rows_in = tokens[order]
        scaled = (gate_row[order][:, None] * grad_f[order]).astype(jnp.bfloat16)
        gate_mat = w_gate[index]
        up_mat = w_up[index]
        down_mat = w_down[index]
        pre_gate = jnp.dot(rows_in, gate_mat, preferred_element_type=jnp.float32)
        pre_up = jnp.dot(rows_in, up_mat, preferred_element_type=jnp.float32)
        grad_hidden = jnp.dot(scaled, down_mat.T, preferred_element_type=jnp.float32)
        squash = jax.nn.sigmoid(pre_gate)
        hidden = (squash * pre_gate * pre_up).astype(jnp.bfloat16)
        grad_a = (grad_hidden * pre_up * squash * (1.0 + pre_gate * (1.0 - squash))).astype(jnp.bfloat16)
        grad_b = (grad_hidden * squash * pre_gate).astype(jnp.bfloat16)
        grad_g = jnp.dot(rows_in.T, grad_a, preferred_element_type=jnp.float32).astype(jnp.bfloat16)
        grad_u = jnp.dot(rows_in.T, grad_b, preferred_element_type=jnp.float32).astype(jnp.bfloat16)
        grad_d = jnp.dot(hidden.T, scaled, preferred_element_type=jnp.float32).astype(jnp.bfloat16)
        partial_rows = jnp.dot(grad_a, gate_mat.T, preferred_element_type=jnp.float32) + jnp.dot(grad_b, up_mat.T, preferred_element_type=jnp.float32)
        partial_rows = jnp.where(picked[order][:, None], partial_rows, jnp.zeros_like(partial_rows))
        grad_acc = grad_acc.at[order].add(partial_rows)
        return grad_acc, (grad_g, grad_u, grad_d)

    start_acc = jnp.zeros(tokens.shape, jnp.float32)
    grad_acc, stacked = lax.scan(one_expert, start_acc, jnp.arange(EXPERTS, dtype=jnp.int32))
    grad_gate, grad_up, grad_down = stacked
    return (grad_acc.astype(jnp.bfloat16), grad_gate, grad_up, grad_down)
```

```python
import functools

import jax
import jax.numpy as jnp
from jax import lax
from jax.experimental import pallas as pl
from jax.experimental.pallas import tpu as pltpu
from jax.sharding import PartitionSpec as P

F32 = jnp.float32
BF16 = jnp.bfloat16
VMEM_LIMIT = 56 * 1024 * 1024


def contract(left, right, left_dim, right_dim):
    return lax.dot_general(
        left, right, (((left_dim,), (right_dim,)), ((), ())), preferred_element_type=F32
    )


def place_kernel(experts, cap, with_gate, *refs):
    if with_gate:
        ids_ref, gate_ref, rows_ref, *outs = refs
    else:
        ids_ref, rows_ref, *outs = refs
    toks = rows_ref.shape[0]
    ids0 = ids_ref[0:1, :]
    ids1 = ids_ref[1:2, :]
    rel = lax.broadcasted_iota(jnp.int32, (experts, toks), 0)
    match = (rel == ids0) | (rel == ids1)
    earlier = (
        lax.broadcasted_iota(jnp.int32, (toks, toks), 0)
        < lax.broadcasted_iota(jnp.int32, (toks, toks), 1)
    ).astype(BF16)
    rank = jnp.dot(match.astype(BF16), earlier, preferred_element_type=F32).astype(jnp.int32)
    rank = jnp.where(match, rank, -1)
    slot = lax.broadcasted_iota(jnp.int32, (cap, toks), 0)
    rows = rows_ref[...]
    for d in range(experts):
        placing = slot == rank[d : d + 1, :]
        block = jnp.dot(placing.astype(BF16), rows, preferred_element_type=F32)
        if with_gate:
            gate = jnp.where(ids0 == d, gate_ref[0:1, :], gate_ref[1:2, :])
            slot_gate = jnp.sum(jnp.where(placing, gate, 0.0), axis=1, keepdims=True)
            block = block * slot_gate
        else:
            outs[experts][d * cap : (d + 1) * cap, :] = placing.astype(BF16)
        outs[d][...] = block.astype(BF16)


def place(ids_rel, rows, experts, cap, gate=None):
    toks, width = rows.shape
    with_gate = gate is not None
    outs = [jax.ShapeDtypeStruct((cap, width), BF16)] * experts
    if not with_gate:
        outs = outs + [jax.ShapeDtypeStruct((experts * cap, toks), BF16)]
    args = (ids_rel, gate, rows) if with_gate else (ids_rel, rows)
    return pl.pallas_call(
        functools.partial(place_kernel, experts, cap, with_gate),
        out_shape=outs,
        name="place_scaled" if with_gate else "place_tokens",
        compiler_params=pltpu.CompilerParams(vmem_limit_bytes=VMEM_LIMIT),
        cost_estimate=pl.CostEstimate(
            flops=2 * experts * cap * toks * width,
            bytes_accessed=2 * width * (toks + experts * cap),
            transcendentals=0,
        ),
    )(*args)


def swap(rows, axis, mask):
    count = lax.axis_size(axis)
    return lax.ppermute(rows, axis, [(i, i ^ mask) for i in range(count)])


def send_order(experts):
    return sorted(range(1, experts), key=lambda d: (-(d >> 1).bit_count(), d))


def body(tokens, grad_out, expert_ids, gate_vals, w_gate, w_up, w_down):
    experts = lax.axis_size("expert")
    dp = lax.axis_size("dp")
    toks, width = tokens.shape
    cap = 3 * toks // experts
    me = lax.axis_index("expert")
    mine = lax.axis_index("dp")
    ids_rel = expert_ids.T ^ me
    *send_x, placing = place(ids_rel, tokens, experts, cap)
    send_r = place(ids_rel, grad_out, experts, cap, gate_vals.T)
    order = send_order(experts)
    recv_x, recv_r = [send_x[0]] * experts, [send_r[0]] * experts
    for d in order:
        recv_x[d] = swap(send_x[d], "expert", d)
    for d in order:
        recv_r[d] = swap(send_r[d], "expert", d)
    recv_x = jnp.concatenate(recv_x, axis=0)
    recv_r = jnp.concatenate(recv_r, axis=0)
    gate_mat, up_mat, down_mat = w_gate[0], w_up[0], w_down[0]
    pre_gate = jnp.dot(recv_x, gate_mat, preferred_element_type=F32)
    pre_up = jnp.dot(recv_x, up_mat, preferred_element_type=F32)
    grad_hidden = contract(recv_r, down_mat, 1, 1)
    squash = jax.nn.sigmoid(pre_gate)
    hidden = (squash * pre_gate * pre_up).astype(BF16)
    grad_a = (grad_hidden * pre_up * squash * (1.0 + pre_gate * (1.0 - squash))).astype(BF16)
    grad_b = (grad_hidden * squash * pre_gate).astype(BF16)
    partial = (contract(grad_a, gate_mat, 1, 1) + contract(grad_b, up_mat, 1, 1)).astype(BF16)
    back = [partial[d * cap : (d + 1) * cap] for d in range(experts)]
    for d in order:
        back[d] = swap(back[d], "expert", d)
    grad_gate = contract(recv_x, grad_a, 0, 0).astype(BF16)
    grad_up = contract(recv_x, grad_b, 0, 0).astype(BF16)
    grad_down = contract(hidden, recv_r, 0, 0).astype(BF16)
    combined = contract(placing, jnp.concatenate(back, axis=0), 0, 0)
    part = width // dp
    total = lax.dynamic_slice_in_dim(combined, mine * part, part, 1)
    for s in range(1, dp):
        other = lax.dynamic_slice_in_dim(combined, (mine ^ s) * part, part, 1)
        total = total + swap(other.astype(BF16), "dp", s).astype(F32)
    return (total.astype(BF16), grad_gate[None], grad_up[None], grad_down[None])


def solution(mesh):
    in_specs = (
        P("expert", None),
        P("expert", None),
        P("expert", None),
        P("expert", None),
        P("expert", None, "dp"),
        P("expert", None, "dp"),
        P("expert", "dp", None),
    )
    out_specs = (
        P("expert", "dp"),
        P("expert", None, "dp"),
        P("expert", None, "dp"),
        P("expert", "dp", None),
    )
    return jax.shard_map(body, mesh=mesh, in_specs=in_specs, out_specs=out_specs, check_vma=False)
```

```python
import functools

import jax
import jax.numpy as jnp
from jax import lax
from jax.experimental import pallas as pl
from jax.experimental.pallas import tpu as pltpu
from jax.sharding import PartitionSpec as P

F32 = jnp.float32
BF16 = jnp.bfloat16
VMEM_LIMIT = 20 * 1024 * 1024
AWAY_FLOPS = 2 * 10**9


def contract(left, right, left_dim, right_dim):
    return lax.dot_general(
        left, right, (((left_dim,), (right_dim,)), ((), ())), preferred_element_type=F32
    )


def like(*shape, dtype=BF16):
    return jax.ShapeDtypeStruct(shape, dtype)


def call(kernel, name, where, args, in_specs, out_shape, out_specs, grid, flops, kept=()):
    moved = sum(a.size * a.dtype.itemsize for a in (*args, *out_shape)) // (2 if kept else 1)
    args = (*kept, *args)
    in_specs = [pl.BlockSpec(memory_space=pl.ANY)] * len(kept) + in_specs

    def inner(where, *refs):
        kernel(where, *refs[len(kept) :])

    return pl.pallas_call(
        inner,
        input_output_aliases={i + 1: i for i in range(len(kept))},
        grid_spec=pltpu.PrefetchScalarGridSpec(
            num_scalar_prefetch=1, grid=grid, in_specs=in_specs, out_specs=out_specs
        ),
        out_shape=out_shape,
        name=name,
        compiler_params=pltpu.CompilerParams(vmem_limit_bytes=VMEM_LIMIT),
        cost_estimate=pl.CostEstimate(flops=flops // 64, bytes_accessed=moved // 64, transcendentals=0),
    )(where, *args)


def whole(array):
    return pl.BlockSpec(array.shape, lambda *_: (0,) * len(array.shape))


class Plan:
    def __init__(self, experts):
        chips = experts // 2
        by_hops = sorted(range(1, chips), key=lambda c: (-c.bit_count(), c))
        self.experts = experts
        self.far = sorted(by_hops[: chips // 2 - 1])
        self.near = sorted(by_hops[chips // 2 - 1 :])
        self.chips = [0] + self.far + self.near


def after(array, *earlier):
    return lax.optimization_barrier((array, *earlier))[0]


def place_kernel(plan, cap, with_gate, where, *refs):
    metas, tables, outs = refs[:2], refs[2:4], refs[4:]
    chips, experts = len(plan.chips), plan.experts
    toks, width = tables[0].shape
    half = pl.ds(pl.multiple_of((where[1] & 1) * (width // 2), 128), width // 2)
    earlier = (
        lax.broadcasted_iota(jnp.int32, (toks, toks), 0)
        < lax.broadcasted_iota(jnp.int32, (toks, toks), 1)
    ).astype(BF16)
    slot = lax.broadcasted_iota(jnp.int32, (cap, toks), 0)
    for side in range(2):
        ids = metas[side][0:2, :].astype(jnp.int32) ^ where[0]
        ids0, ids1 = ids[0:1, :], ids[1:2, :]
        rel = lax.broadcasted_iota(jnp.int32, (experts, toks), 0)
        match = (rel == ids0) | (rel == ids1)
        rank = jnp.dot(match.astype(BF16), earlier, preferred_element_type=F32).astype(jnp.int32)
        rank = jnp.where(match, rank, -1)
        for place, chip in enumerate(plan.chips):
            d = 2 * chip
            placing = slot == rank[d : d + 1, :]
            rows = tables[side][:, half] if chip in plan.far else tables[side][...]
            block = jnp.dot(placing.astype(BF16), rows, preferred_element_type=F32)
            if with_gate:
                gate = jnp.where(ids0 == d, metas[side][2:3, :], metas[side][3:4, :])
                slot_gate = jnp.sum(jnp.where(placing, gate, 0.0), axis=1, keepdims=True)
                block = block * slot_gate
            else:
                outs[chips + side][place * cap : (place + 1) * cap, :] = placing.astype(BF16)
            outs[chip][side * cap : (side + 1) * cap, :] = block.astype(BF16)


def place(plan, where, metas, tables, cap, with_gate):
    toks, width = tables[0].shape
    chips = len(plan.chips)
    outs = [like(2 * cap, width // 2 if c in plan.far else width) for c in range(chips)]
    if not with_gate:
        outs = outs + [like(chips * cap, toks)] * 2
    args = (*metas, *tables)
    return call(
        functools.partial(place_kernel, plan, cap, with_gate),
        "place_scaled" if with_gate else "place_tokens",
        where,
        args,
        [whole(a) for a in args],
        outs,
        [whole(o) for o in outs],
        (1,),
        2 * plan.experts * cap * toks * width,
    )


def gather_blocks(where, out_ref, full, halves, others):
    cap = full[0].shape[0]
    width = out_ref.shape[1]
    part = width // 2
    for i, block in enumerate(full):
        out_ref[i * cap : (i + 1) * cap, :] = block[...]
    if not halves:
        return
    mine = pl.ds(pl.multiple_of((where[1] & 1) * part, 128), part)
    theirs = pl.ds(pl.multiple_of((1 - (where[1] & 1)) * part, 128), part)
    base = len(full) * cap
    for i, block in enumerate(halves):
        out_ref[base + i * cap : base + (i + 1) * cap, mine] = block[...]
    out_ref[base : base + len(halves) * cap, theirs] = others[...]


def split_refs(refs, n_full, n_halves):
    full = refs[:n_full]
    halves = refs[n_full : n_full + n_halves]
    rest = refs[n_full + n_halves :]
    if n_halves:
        return full, halves, rest[0], rest[1:]
    return full, halves, None, rest


def forward_kernel(n_full, n_halves, where, *refs):
    full, halves, others, rest = split_refs(refs, n_full, n_halves)
    gate_ref, up_ref, rows_ref, hidden_ref, to_a_ref, to_b_ref = rest

    @pl.when(pl.program_id(0) == 0)
    def _():
        gather_blocks(where, rows_ref, full, halves, others)

    rows = rows_ref[...]
    pre_gate = jnp.dot(rows, gate_ref[0], preferred_element_type=F32)
    pre_up = jnp.dot(rows, up_ref[0], preferred_element_type=F32)
    squash = jax.nn.sigmoid(pre_gate)
    swish = squash * pre_gate
    hidden_ref[...] = (swish * pre_up).astype(BF16)
    to_a_ref[...] = pre_up * squash * (1.0 + pre_gate * (1.0 - squash))
    to_b_ref[...] = swish


def forward(name, where, chunk, full, halves, others, w_gate, w_up, kept=()):
    cap, width = full[0].shape
    count = (len(full) + len(halves)) * cap
    rows = 2 * count
    units = w_gate.shape[2]
    tile = 256
    blocks = [*full, *halves, *others]
    column = pl.BlockSpec((1, width, tile), lambda j, _: (0, 0, j))
    out_column = pl.BlockSpec((count, tile), lambda j, _: (0, j))
    outs = [
        like(rows, width),
        like(rows, units),
        like(count, units, dtype=F32),
        like(count, units, dtype=F32),
    ]
    return call(
        functools.partial(forward_kernel, len(full), len(halves)),
        name,
        where,
        (*blocks, w_gate, w_up),
        [whole(b) for b in blocks] + [column, column],
        outs,
        [
            pl.BlockSpec((count, width), lambda j, _: (chunk, 0)),
            pl.BlockSpec((count, tile), lambda j, _: (chunk, j)),
            out_column,
            out_column,
        ],
        (units // tile,),
        4 * count * width * units,
        kept,
    )


def backward_kernel(n_full, n_halves, where, *refs):
    full, halves, others, rest = split_refs(refs, n_full, n_halves)
    down_ref, to_a_ref, to_b_ref, rows_ref, grad_a_ref, grad_b_ref = rest

    @pl.when(pl.program_id(0) == 0)
    def _():
        gather_blocks(where, rows_ref, full, halves, others)

    grad_hidden = contract(rows_ref[...], down_ref[0], 1, 1)
    grad_a_ref[...] = (grad_hidden * to_a_ref[...]).astype(BF16)
    grad_b_ref[...] = (grad_hidden * to_b_ref[...]).astype(BF16)


def backward(name, where, chunk, full, halves, others, w_down, to_a, to_b, kept=()):
    cap, width = full[0].shape
    count = (len(full) + len(halves)) * cap
    rows = 2 * count
    units = w_down.shape[1]
    tile = 256
    blocks = [*full, *halves, *others]
    column = pl.BlockSpec((count, tile), lambda j, _: (0, j))
    out_column = pl.BlockSpec((count, tile), lambda j, _: (chunk, j))
    outs = [like(rows, width), like(rows, units), like(rows, units)]
    return call(
        functools.partial(backward_kernel, len(full), len(halves)),
        name,
        where,
        (*blocks, w_down, to_a, to_b),
        [whole(b) for b in blocks]
        + [pl.BlockSpec((1, tile, width), lambda j, _: (0, j, 0)), column, column],
        outs,
        [pl.BlockSpec((count, width), lambda j, _: (chunk, 0)), out_column, out_column],
        (units // tile,),
        2 * count * width * units,
        kept,
    )


def input_grad(grad_a_ref, grad_b_ref, gate_ref, up_ref):
    return contract(grad_a_ref[...], gate_ref[0], 1, 1) + contract(
        grad_b_ref[...], up_ref[0], 1, 1
    )


def first_grad_kernel(cap, where, grad_a_ref, grad_b_ref, gate_ref, up_ref, *outs):
    own_ref, give_ref, keep_ref = outs
    part = input_grad(grad_a_ref, grad_b_ref, gate_ref, up_ref)
    own_ref[...] = part[: 2 * cap].astype(BF16)
    far = part[2 * cap :]
    step, steps = pl.program_id(0), pl.num_programs(0)

    @pl.when(step < steps // 2)
    def _():
        give_ref[...] = far.astype(BF16)

    @pl.when(step >= steps // 2)
    def _():
        keep_ref[...] = far


def first_grad(plan, where, grad_a, grad_b, w_gate, w_up, dp, cap):
    width, units = w_gate.shape[1:]
    slab = width // dp
    far = 2 * len(plan.far) * cap

    def at(i, where):
        parity = where[1] & 1
        late = jnp.where(i < dp // 2, 1 - parity, parity)
        return 2 * lax.rem(i, dp // 2) + late

    weight = pl.BlockSpec((1, slab, units), lambda i, where: (0, at(i, where), 0))
    chunk = pl.BlockSpec((grad_a.shape[0] // 2, units), lambda i, where: (0, 0))
    outs = [
        like(2 * cap, width),
        like(far, width // 2),
        like(far, width // 2, dtype=F32),
    ]
    return call(
        functools.partial(first_grad_kernel, cap),
        "own_and_far_input_grads",
        where,
        (grad_a, grad_b, w_gate, w_up),
        [chunk, chunk, weight, weight],
        outs,
        [
            pl.BlockSpec((2 * cap, slab), lambda i, where: (0, at(i, where))),
            pl.BlockSpec((far, slab), lambda i, where: (0, jnp.minimum(i, dp // 2 - 1))),
            pl.BlockSpec((far, slab), lambda i, where: (0, jnp.maximum(i - dp // 2, 0))),
        ],
        (dp,),
        2 * grad_a.shape[0] * width * units,
    )


def near_grad_kernel(cap, where, grad_a_ref, grad_b_ref, gate_ref, up_ref, *outs):
    part = input_grad(grad_a_ref, grad_b_ref, gate_ref, up_ref)
    for i, out in enumerate(outs):
        out[...] = part[2 * i * cap : 2 * (i + 1) * cap].astype(BF16)


def near_grad(plan, where, grad_a, grad_b, w_gate, w_up, dp, cap, away):
    width, units = w_gate.shape[1:]
    tile = width // 4
    steps = 2

    def at(i, where):
        side = (where[1] >= dp // 2).astype(jnp.int32)
        return steps * (1 - side if away else side) + i

    weight = pl.BlockSpec((1, tile, units), lambda i, where: (0, at(i, where), 0))
    chunk = pl.BlockSpec((grad_a.shape[0] // 2, units), lambda i, where: (1, 0))
    outs = [like(2 * cap, width // 2)] * len(plan.near)
    return call(
        functools.partial(near_grad_kernel, cap),
        "near_input_grads",
        where,
        (grad_a, grad_b, w_gate, w_up),
        [chunk, chunk, weight, weight],
        outs,
        [pl.BlockSpec((2 * cap, tile), lambda i, where: (0, i))] * len(plan.near),
        (steps,),
        grad_a.shape[0] * width * units,
    )


def outer_kernel(n_right, where, left_ref, *refs):
    left = left_ref[...].T
    for right, out in zip(refs[:n_right], refs[n_right:], strict=True):
        out[0] = jnp.dot(left, right[...], preferred_element_type=F32).astype(BF16)


def outer(name, where, left, rights, part=0, parts=1, kept=()):
    rows, width = left.shape
    tile = 256
    steps = width // tile // parts
    first = part * steps
    outs = [like(1, width, r.shape[1]) for r in rights]
    return call(
        functools.partial(outer_kernel, len(rights)),
        name,
        where,
        (left, *rights),
        [pl.BlockSpec((rows, tile), lambda i, _: (0, first + i))] + [whole(r) for r in rights],
        outs,
        [pl.BlockSpec((1, tile, o.shape[2]), lambda i, _: (0, first + i, 0)) for o in outs],
        (steps,),
        2 * rows * width * sum(o.shape[2] for o in outs) // parts,
        kept,
    )


def combine_kernel(plan, cap, dp, shifts, side_by_side, where, *refs):
    chips = len(plan.chips)
    placings, blocks, outs, rows_ref = refs[:2], refs[2 : 2 + chips], refs[2 + chips : -1], refs[-1]
    slab = rows_ref.shape[1]
    side_rows = chips * cap
    for n, shift in enumerate(shifts):
        to = where[1] ^ shift
        for place, (chip, block) in enumerate(zip(plan.chips, blocks, strict=True)):
            if chip == 0:
                column = to
            elif chip in plan.far:
                column = to >> 1
            else:
                column = lax.rem(to, dp // 2)
            column = pl.ds(pl.multiple_of(column * slab, 128), slab)
            for side in range(2):
                base = side * side_rows + place * cap
                if chip in plan.far and shift % 2:
                    rows_ref[base : base + cap, :] = jnp.zeros((cap, slab), BF16)
                else:
                    rows_ref[base : base + cap, :] = block[side * cap : (side + 1) * cap, column]
        own = contract(placings[0][...], rows_ref[:side_rows, :], 0, 0)
        other = contract(placings[1][...], rows_ref[side_rows:, :], 0, 0)
        if side_by_side:
            outs[0][:, n * slab : (n + 1) * slab] = own
            outs[1][:, n * slab : (n + 1) * slab] = other.astype(BF16)
        else:
            outs[2 * n][...] = own.astype(outs[2 * n].dtype)
            outs[2 * n + 1][...] = other.astype(BF16)


def combine(plan, where, placings, blocks, dp, cap, shifts, side_by_side):
    width = blocks[0].shape[1]
    slab = width // dp
    toks = placings[0].shape[1]
    args = (*placings, *blocks)
    if side_by_side:
        outs = [like(toks, slab * len(shifts), dtype=F32), like(toks, slab * len(shifts))]
    else:
        pairs = [[like(toks, slab, dtype=BF16 if s else F32), like(toks, slab)] for s in shifts]
        outs = [o for pair in pairs for o in pair]
    moved = sum(a.size * a.dtype.itemsize for a in args)
    flops = 4 * placings[0].size * slab * len(shifts)
    return pl.pallas_call(
        functools.partial(combine_kernel, plan, cap, dp, shifts, side_by_side),
        grid_spec=pltpu.PrefetchScalarGridSpec(
            num_scalar_prefetch=1,
            grid=(1,),
            in_specs=[whole(a) for a in args],
            out_specs=[whole(o) for o in outs],
            scratch_shapes=[pltpu.VMEM((plan.experts * cap, slab), BF16)],
        ),
        out_shape=outs,
        name="combine_away" if side_by_side else "combine_here",
        compiler_params=pltpu.CompilerParams(vmem_limit_bytes=VMEM_LIMIT),
        cost_estimate=pl.CostEstimate(
            flops=flops // 64, bytes_accessed=moved // 64, transcendentals=0
        ),
    )(where, *args)


def sum_kernel(*refs):
    *parts, out = refs
    out[...] = functools.reduce(lambda a, b: a + b, [p[...].astype(F32) for p in parts])


def add_up(parts):
    out = like(*parts[0].shape, dtype=F32)
    return pl.pallas_call(
        sum_kernel,
        out_shape=out,
        name="add_up",
        compiler_params=pltpu.CompilerParams(vmem_limit_bytes=VMEM_LIMIT),
        cost_estimate=pl.CostEstimate(
            flops=AWAY_FLOPS, bytes_accessed=2 * out.size, transcendentals=0
        ),
    )(*parts)


def swap(rows, axis, mask):
    count = lax.axis_size(axis)
    return lax.ppermute(rows, axis, [(i, i ^ mask) for i in range(count)])


def cross(rows, shift):
    dp = lax.axis_size("dp")
    count = lax.axis_size("expert") * dp
    return lax.ppermute(rows, ("expert", "dp"), [(i, i ^ (dp + shift)) for i in range(count)])


def body(tokens, grad_out, expert_ids, gate_vals, w_gate, w_up, w_down):
    plan = Plan(lax.axis_size("expert"))
    dp = lax.axis_size("dp")
    toks, width = tokens.shape
    cap = 3 * toks // plan.experts
    where = jnp.stack([lax.axis_index("expert"), lax.axis_index("dp")]).astype(jnp.int32)
    meta = jnp.concatenate([expert_ids.T.astype(F32), gate_vals.T], axis=0)
    meta_other = swap(meta, "expert", 1)
    tokens_other = swap(tokens, "expert", 1)
    out_other = swap(grad_out, "expert", 1)
    metas = (meta, meta_other)
    *x, placing, placing_other = place(plan, where, metas, (tokens, tokens_other), cap, False)
    r = list(place(plan, where, metas, (grad_out, out_other), cap, True))
    placings = (placing, placing_other)

    def over(blocks, which):
        for c in which:
            blocks[c] = swap(blocks[c], "expert", 2 * c)

    def share(blocks):
        return [swap(jnp.concatenate([blocks[c] for c in plan.far], axis=0), "dp", 1)]

    def pick(blocks, which):
        return [blocks[c] for c in which]

    over(x, plan.far)
    over(r, plan.far)
    x_others, r_others = share(x), share(r)
    over(x, plan.near)
    for c in plan.near:
        r[c] = after(r[c], *x_others)
    over(r, plan.near)

    x_all, hidden, to_a, to_b = forward(
        "forward_own_and_far", where, 0, pick(x, [0]), pick(x, plan.far), x_others, w_gate, w_up
    )
    r_all, grad_a, grad_b = backward(
        "backward_own_and_far", where, 0, pick(r, [0]), pick(r, plan.far), r_others, w_down, to_a, to_b
    )
    own, give, keep = first_grad(plan, where, grad_a, grad_b, w_gate, w_up, dp, cap)
    got = swap(give, "dp", 1)

    x_all, hidden, to_a, to_b = forward(
        "forward_near", where, 1, pick(x, plan.near), [], [], w_gate, w_up, (after(x_all, give), hidden)
    )
    far_sum = (keep + after(got, hidden, *pick(r, plan.near)).astype(F32)).astype(BF16)
    rows = 2 * cap
    far = [swap(far_sum[i * rows : (i + 1) * rows], "expert", 2 * c) for i, c in enumerate(plan.far)]
    kept = (after(r_all, far_sum), after(grad_a, give), after(grad_b, give))
    r_all, grad_a, grad_b = backward(
        "backward_near", where, 1, pick(r, plan.near), [], [], w_down, to_a, to_b, kept
    )
    away_part = near_grad(plan, where, grad_a, grad_b, w_gate, w_up, dp, cap, True)
    here_part = near_grad(plan, where, after(grad_a, *far), grad_b, w_gate, w_up, dp, cap, False)

    def send_back(part):
        return [swap(b, "expert", 2 * c) for b, c in zip(part, plan.near, strict=True)]

    away_rows, here_rows = send_back(away_part), send_back(here_part)
    slab = width // dp
    away, here = list(range(dp // 2, dp)), list(range(dp // 2))

    (grad_down,) = outer("down_grad", where, after(hidden, here_part[0]), [r_all])
    away_rows[0] = after(away_rows[0], grad_down)
    away_sum, other = combine(
        plan, where, placings, [own, *far, *away_rows], dp, cap, away, True
    )
    other = swap(other, "expert", 1)
    grads = outer("gate_and_up_grads", where, after(x_all, away_sum), [grad_a, grad_b], 0, 4)
    away_sum = (away_sum + after(other, grads[0]).astype(F32)).astype(BF16)
    parts = [away_sum[:, n * slab : (n + 1) * slab] for n in range(len(away))]
    grads = outer("gate_and_up_grads", where, after(x_all, *parts), [grad_a, grad_b], 1, 4, grads)
    away_sums = [swap(part, "dp", s) for part, s in zip(parts, away, strict=True)]
    here_rows[0] = after(here_rows[0], grads[0])
    total, other, *rest = combine(
        plan, where, placings, [own, *far, *here_rows], dp, cap, here, False
    )
    got = [swap(other, "expert", 1)]
    for n, s in enumerate(here[1:]):
        got += [swap(rest[2 * n], "dp", s), cross(rest[2 * n + 1], s)]
    grads = outer("gate_and_up_grads", where, after(x_all, total), [grad_a, grad_b], 2, 4, grads)
    grad_gate, grad_up = outer("gate_and_up_grads", where, x_all, [grad_a, grad_b], 3, 4, grads)
    total = total + add_up(away_sums)
    for part in got:
        total = total + part.astype(F32)
    return (total.astype(BF16), grad_gate, grad_up, grad_down)


def solution(mesh):
    in_specs = (
        P("expert", None),
        P("expert", None),
        P("expert", None),
        P("expert", None),
        P("expert", None, "dp"),
        P("expert", None, "dp"),
        P("expert", "dp", None),
    )
    out_specs = (
        P("expert", "dp"),
        P("expert", None, "dp"),
        P("expert", None, "dp"),
        P("expert", "dp", None),
    )
    return jax.shard_map(body, mesh=mesh, in_specs=in_specs, out_specs=out_specs, check_vma=False)
```

```python
import functools

import jax
import jax.numpy as jnp
from jax import lax
from jax.experimental import pallas as pl
from jax.experimental.pallas import tpu as pltpu
from jax.sharding import PartitionSpec as P

F32 = jnp.float32
BF16 = jnp.bfloat16
VMEM_LIMIT = 20 * 1024 * 1024
COST = {"forward_near": 60000, "backward_near": 1000, "own_and_far_input_grads": 100, "near_grads_away": 20000, "near_grads_here": 100, "gate_and_up_0": 1000, "gate_and_up_1": 5000, "gate_and_up_2": 20000, "gate_and_up_3": 20000, "combine_away": 20000, "combine_here": 20000, "place_tokens": 100}
COST = {name: 10**6 * cost for name, cost in COST.items()}
LATE_QUARTER = True
FAR_FIRST = 'here'
SIDE_LAST = 'core'


def contract(left, right, left_dim, right_dim):
    return lax.dot_general(
        left, right, (((left_dim,), (right_dim,)), ((), ())), preferred_element_type=F32
    )


def like(*shape, dtype=BF16):
    return jax.ShapeDtypeStruct(shape, dtype)


def estimate(name):
    return pl.CostEstimate(flops=COST.get(name, 0), bytes_accessed=0, transcendentals=0)


def call(kernel, name, where, args, in_specs, out_shape, out_specs, grid, kept=()):
    args = (*kept, *args)
    in_specs = [pl.BlockSpec(memory_space=pl.ANY)] * len(kept) + in_specs

    def inner(where, *refs):
        kernel(where, *refs[len(kept) :])

    return pl.pallas_call(
        inner,
        input_output_aliases={i + 1: i for i in range(len(kept))},
        grid_spec=pltpu.PrefetchScalarGridSpec(
            num_scalar_prefetch=1, grid=grid, in_specs=in_specs, out_specs=out_specs
        ),
        out_shape=out_shape,
        name=name,
        compiler_params=pltpu.CompilerParams(vmem_limit_bytes=VMEM_LIMIT),
        cost_estimate=estimate(name),
    )(where, *args)


def whole(array):
    return pl.BlockSpec(array.shape, lambda *_: (0,) * len(array.shape))


class Plan:
    def __init__(self, experts):
        chips = experts // 2
        by_hops = sorted(range(1, chips), key=lambda c: (-c.bit_count(), c))
        self.experts = experts
        self.far = sorted(by_hops[: chips // 2 - 1])
        self.near = sorted(by_hops[chips // 2 - 1 :])
        self.chips = [0] + self.far + self.near


def after(array, *earlier):
    return lax.optimization_barrier((array, *earlier))[0]


def place_kernel(plan, cap, with_gate, chips, placings, where, *refs):
    metas, tables, outs = refs[:2], refs[2:4], refs[4:]
    experts = plan.experts
    toks, width = tables[0].shape
    half = pl.ds(pl.multiple_of((where[1] & 1) * (width // 2), 128), width // 2)
    earlier = (
        lax.broadcasted_iota(jnp.int32, (toks, toks), 0)
        < lax.broadcasted_iota(jnp.int32, (toks, toks), 1)
    ).astype(BF16)
    slot = lax.broadcasted_iota(jnp.int32, (cap, toks), 0)
    for side in range(2):
        ids = metas[side][0:2, :].astype(jnp.int32) ^ where[0]
        ids0, ids1 = ids[0:1, :], ids[1:2, :]
        rel = lax.broadcasted_iota(jnp.int32, (experts, toks), 0)
        match = (rel == ids0) | (rel == ids1)
        rank = jnp.dot(match.astype(BF16), earlier, preferred_element_type=F32).astype(jnp.int32)
        rank = jnp.where(match, rank, -1)
        for place, chip in enumerate(plan.chips):
            d = 2 * chip
            placing = slot == rank[d : d + 1, :]
            if placings:
                outs[len(chips) + side][place * cap : (place + 1) * cap, :] = placing.astype(BF16)
            if chip not in chips:
                continue
            rows = tables[side][:, half] if chip in plan.far else tables[side][...]
            block = jnp.dot(placing.astype(BF16), rows, preferred_element_type=F32)
            if with_gate:
                gate = jnp.where(ids0 == d, metas[side][2:3, :], metas[side][3:4, :])
                slot_gate = jnp.sum(jnp.where(placing, gate, 0.0), axis=1, keepdims=True)
                block = block * slot_gate
            outs[chips.index(chip)][side * cap : (side + 1) * cap, :] = block.astype(BF16)


def place(name, plan, where, metas, tables, cap, with_gate, chips, placings=False):
    toks, width = tables[0].shape
    outs = [like(2 * cap, width // 2 if c in plan.far else width) for c in chips]
    if placings:
        outs = outs + [like(len(plan.chips) * cap, toks)] * 2
    args = (*metas, *tables)
    return call(
        functools.partial(place_kernel, plan, cap, with_gate, chips, placings),
        name,
        where,
        args,
        [whole(a) for a in args],
        outs,
        [whole(o) for o in outs],
        (1,),
    )


def gather_blocks(where, out_ref, full, halves, others):
    cap = full[0].shape[0]
    width = out_ref.shape[1]
    part = width // 2
    for i, block in enumerate(full):
        out_ref[i * cap : (i + 1) * cap, :] = block[...]
    if not halves:
        return
    mine = pl.ds(pl.multiple_of((where[1] & 1) * part, 128), part)
    theirs = pl.ds(pl.multiple_of((1 - (where[1] & 1)) * part, 128), part)
    base = len(full) * cap
    for i, block in enumerate(halves):
        out_ref[base + i * cap : base + (i + 1) * cap, mine] = block[...]
    out_ref[base : base + len(halves) * cap, theirs] = others[...]


def split_refs(refs, n_full, n_halves):
    full = refs[:n_full]
    halves = refs[n_full : n_full + n_halves]
    rest = refs[n_full + n_halves :]
    if n_halves:
        return full, halves, rest[0], rest[1:]
    return full, halves, None, rest


def forward_kernel(n_full, n_halves, where, *refs):
    full, halves, others, rest = split_refs(refs, n_full, n_halves)
    gate_ref, up_ref, rows_ref, hidden_ref, to_a_ref, to_b_ref = rest

    @pl.when(pl.program_id(0) == 0)
    def _():
        gather_blocks(where, rows_ref, full, halves, others)

    rows = rows_ref[...]
    pre_gate = jnp.dot(rows, gate_ref[0], preferred_element_type=F32)
    pre_up = jnp.dot(rows, up_ref[0], preferred_element_type=F32)
    squash = jax.nn.sigmoid(pre_gate)
    swish = squash * pre_gate
    hidden_ref[...] = (swish * pre_up).astype(BF16)
    to_a_ref[...] = pre_up * squash * (1.0 + pre_gate * (1.0 - squash))
    to_b_ref[...] = swish


def forward(name, where, chunk, full, halves, others, w_gate, w_up, kept=()):
    cap, width = full[0].shape
    count = (len(full) + len(halves)) * cap
    rows = 2 * count
    units = w_gate.shape[2]
    tile = 256
    blocks = [*full, *halves, *others]
    column = pl.BlockSpec((1, width, tile), lambda j, _: (0, 0, j))
    out_column = pl.BlockSpec((count, tile), lambda j, _: (0, j))
    outs = [
        like(rows, width),
        like(rows, units),
        like(count, units, dtype=F32),
        like(count, units, dtype=F32),
    ]
    return call(
        functools.partial(forward_kernel, len(full), len(halves)),
        name,
        where,
        (*blocks, w_gate, w_up),
        [whole(b) for b in blocks] + [column, column],
        outs,
        [
            pl.BlockSpec((count, width), lambda j, _: (chunk, 0)),
            pl.BlockSpec((count, tile), lambda j, _: (chunk, j)),
            out_column,
            out_column,
        ],
        (units // tile,),
        kept,
    )


def backward_kernel(n_full, n_halves, where, *refs):
    full, halves, others, rest = split_refs(refs, n_full, n_halves)
    down_ref, to_a_ref, to_b_ref, rows_ref, grad_a_ref, grad_b_ref = rest

    @pl.when(pl.program_id(0) == 0)
    def _():
        gather_blocks(where, rows_ref, full, halves, others)

    grad_hidden = contract(rows_ref[...], down_ref[0], 1, 1)
    grad_a_ref[...] = (grad_hidden * to_a_ref[...]).astype(BF16)
    grad_b_ref[...] = (grad_hidden * to_b_ref[...]).astype(BF16)


def backward(name, where, chunk, full, halves, others, w_down, to_a, to_b, kept=()):
    cap, width = full[0].shape
    count = (len(full) + len(halves)) * cap
    rows = 2 * count
    units = w_down.shape[1]
    tile = 256
    blocks = [*full, *halves, *others]
    column = pl.BlockSpec((count, tile), lambda j, _: (0, j))
    out_column = pl.BlockSpec((count, tile), lambda j, _: (chunk, j))
    outs = [like(rows, width), like(rows, units), like(rows, units)]
    return call(
        functools.partial(backward_kernel, len(full), len(halves)),
        name,
        where,
        (*blocks, w_down, to_a, to_b),
        [whole(b) for b in blocks]
        + [pl.BlockSpec((1, tile, width), lambda j, _: (0, j, 0)), column, column],
        outs,
        [pl.BlockSpec((count, width), lambda j, _: (chunk, 0)), out_column, out_column],
        (units // tile,),
        kept,
    )


def input_grad(grad_a_ref, grad_b_ref, gate_ref, up_ref):
    return contract(grad_a_ref[...], gate_ref[0], 1, 1) + contract(
        grad_b_ref[...], up_ref[0], 1, 1
    )


def first_grad_kernel(cap, where, grad_a_ref, grad_b_ref, gate_ref, up_ref, *outs):
    own_ref, give_ref, keep_ref = outs
    part = input_grad(grad_a_ref, grad_b_ref, gate_ref, up_ref)
    own_ref[...] = part[: 2 * cap].astype(BF16)
    far = part[2 * cap :]
    step, steps = pl.program_id(0), pl.num_programs(0)

    @pl.when(step < steps // 2)
    def _():
        give_ref[...] = far.astype(BF16)

    @pl.when(step >= steps // 2)
    def _():
        keep_ref[...] = far


def first_grad(plan, where, grad_a, grad_b, w_gate, w_up, dp, cap):
    width, units = w_gate.shape[1:]
    slab = width // dp
    far = 2 * len(plan.far) * cap

    def at(i, where):
        parity = where[1] & 1
        late = jnp.where(i < dp // 2, 1 - parity, parity)
        return 2 * lax.rem(i, dp // 2) + late

    weight = pl.BlockSpec((1, slab, units), lambda i, where: (0, at(i, where), 0))
    chunk = pl.BlockSpec((grad_a.shape[0] // 2, units), lambda i, where: (0, 0))
    outs = [
        like(2 * cap, width),
        like(far, width // 2),
        like(far, width // 2, dtype=F32),
    ]
    return call(
        functools.partial(first_grad_kernel, cap),
        "own_and_far_input_grads",
        where,
        (grad_a, grad_b, w_gate, w_up),
        [chunk, chunk, weight, weight],
        outs,
        [
            pl.BlockSpec((2 * cap, slab), lambda i, where: (0, at(i, where))),
            pl.BlockSpec((far, slab), lambda i, where: (0, jnp.minimum(i, dp // 2 - 1))),
            pl.BlockSpec((far, slab), lambda i, where: (0, jnp.maximum(i - dp // 2, 0))),
        ],
        (dp,),
    )


def near_grad_kernel(cap, where, grad_a_ref, grad_b_ref, gate_ref, up_ref, *outs):
    part = input_grad(grad_a_ref, grad_b_ref, gate_ref, up_ref)
    for i, out in enumerate(outs):
        out[...] = part[2 * i * cap : 2 * (i + 1) * cap].astype(BF16)


def near_grad(plan, where, grad_a, grad_b, w_gate, w_up, dp, cap, away):
    width, units = w_gate.shape[1:]
    tile = width // 4
    steps = 2

    def at(i, where):
        side = (where[1] >= dp // 2).astype(jnp.int32)
        return steps * (1 - side if away else side) + i

    weight = pl.BlockSpec((1, tile, units), lambda i, where: (0, at(i, where), 0))
    chunk = pl.BlockSpec((grad_a.shape[0] // 2, units), lambda i, where: (1, 0))
    outs = [like(2 * cap, width // 2)] * len(plan.near)
    return call(
        functools.partial(near_grad_kernel, cap),
        "near_grads_away" if away else "near_grads_here",
        where,
        (grad_a, grad_b, w_gate, w_up),
        [chunk, chunk, weight, weight],
        outs,
        [pl.BlockSpec((2 * cap, tile), lambda i, where: (0, i))] * len(plan.near),
        (steps,),
    )


def outer_kernel(n_right, where, left_ref, *refs):
    left = left_ref[...].T
    for right, out in zip(refs[:n_right], refs[n_right:], strict=True):
        out[0] = jnp.dot(left, right[...], preferred_element_type=F32).astype(BF16)


def outer(name, where, left, rights, part=0, parts=1, kept=()):
    rows, width = left.shape
    tile = 256
    steps = width // tile // parts
    first = part * steps
    outs = [like(1, width, r.shape[1]) for r in rights]
    return call(
        functools.partial(outer_kernel, len(rights)),
        name,
        where,
        (left, *rights),
        [pl.BlockSpec((rows, tile), lambda i, _: (0, first + i))] + [whole(r) for r in rights],
        outs,
        [pl.BlockSpec((1, tile, o.shape[2]), lambda i, _: (0, first + i, 0)) for o in outs],
        (steps,),
        kept,
    )


def combine_kernel(plan, cap, dp, shifts, side_by_side, where, *refs):
    chips = len(plan.chips)
    placings, blocks, outs, rows_ref = refs[:2], refs[2 : 2 + chips], refs[2 + chips : -1], refs[-1]
    slab = rows_ref.shape[1]
    side_rows = chips * cap
    for n, shift in enumerate(shifts):
        to = where[1] ^ shift
        for place, (chip, block) in enumerate(zip(plan.chips, blocks, strict=True)):
            if chip == 0:
                column = to
            elif chip in plan.far:
                column = to >> 1
            else:
                column = lax.rem(to, dp // 2)
            column = pl.ds(pl.multiple_of(column * slab, 128), slab)
            for side in range(2):
                base = side * side_rows + place * cap
                if chip in plan.far and shift % 2:
                    rows_ref[base : base + cap, :] = jnp.zeros((cap, slab), BF16)
                else:
                    rows_ref[base : base + cap, :] = block[side * cap : (side + 1) * cap, column]
        own = contract(placings[0][...], rows_ref[:side_rows, :], 0, 0)
        other = contract(placings[1][...], rows_ref[side_rows:, :], 0, 0)
        if side_by_side:
            outs[0][:, n * slab : (n + 1) * slab] = own
            outs[1][:, n * slab : (n + 1) * slab] = other.astype(BF16)
        else:
            outs[2 * n][...] = own.astype(outs[2 * n].dtype)
            outs[2 * n + 1][...] = other.astype(BF16)


def combine(plan, where, placings, blocks, dp, cap, shifts, side_by_side):
    width = blocks[0].shape[1]
    slab = width // dp
    toks = placings[0].shape[1]
    args = (*placings, *blocks)
    if side_by_side:
        outs = [like(toks, slab * len(shifts), dtype=F32), like(toks, slab * len(shifts))]
    else:
        pairs = [[like(toks, slab, dtype=BF16 if s else F32), like(toks, slab)] for s in shifts]
        outs = [o for pair in pairs for o in pair]
    moved = sum(a.size * a.dtype.itemsize for a in args)
    flops = 4 * placings[0].size * slab * len(shifts)
    return pl.pallas_call(
        functools.partial(combine_kernel, plan, cap, dp, shifts, side_by_side),
        grid_spec=pltpu.PrefetchScalarGridSpec(
            num_scalar_prefetch=1,
            grid=(1,),
            in_specs=[whole(a) for a in args],
            out_specs=[whole(o) for o in outs],
            scratch_shapes=[pltpu.VMEM((plan.experts * cap, slab), BF16)],
        ),
        out_shape=outs,
        name="combine_away" if side_by_side else "combine_here",
        compiler_params=pltpu.CompilerParams(vmem_limit_bytes=VMEM_LIMIT),
        cost_estimate=pl.CostEstimate(
            flops=0, bytes_accessed=0, transcendentals=0
        ),
    )(where, *args)


def sum_kernel(*refs):
    *parts, out = refs
    out[...] = functools.reduce(lambda a, b: a + b, [p[...].astype(F32) for p in parts])


def add_up(parts):
    out = like(*parts[0].shape, dtype=F32)
    return pl.pallas_call(
        sum_kernel,
        out_shape=out,
        name="add_up",
        compiler_params=pltpu.CompilerParams(vmem_limit_bytes=VMEM_LIMIT),
        cost_estimate=estimate("add_up"),
    )(*parts)


def swap(rows, axis, mask):
    count = lax.axis_size(axis)
    return lax.ppermute(rows, axis, [(i, i ^ mask) for i in range(count)])


def cross(rows, shift):
    dp = lax.axis_size("dp")
    count = lax.axis_size("expert") * dp
    return lax.ppermute(rows, ("expert", "dp"), [(i, i ^ (dp + shift)) for i in range(count)])


def body(tokens, grad_out, expert_ids, gate_vals, w_gate, w_up, w_down):
    plan = Plan(lax.axis_size("expert"))
    dp = lax.axis_size("dp")
    toks, width = tokens.shape
    cap = 3 * toks // plan.experts
    where = jnp.stack([lax.axis_index("expert"), lax.axis_index("dp")]).astype(jnp.int32)
    meta = jnp.concatenate([expert_ids.T.astype(F32), gate_vals.T], axis=0)
    meta_other = swap(meta, "expert", 1)
    tokens_other = swap(tokens, "expert", 1)
    out_other = swap(grad_out, "expert", 1)
    metas = (meta, meta_other)
    tables = (pltpu.with_memory_space_constraint(tokens, pltpu.HBM), tokens_other)
    x = [None] * len(plan.chips)
    blocks = place("place_far_tokens", plan, where, metas, tables, cap, False, plan.far)
    for c, block in zip(plan.far, blocks, strict=True):
        x[c] = block
    rest = [0] + plan.near
    metas = (after(meta, x[plan.far[-1]]), meta_other)
    *blocks, placing, placing_other = place(
        "place_tokens", plan, where, metas, tables, cap, False, rest, True
    )
    for c, block in zip(rest, blocks, strict=True):
        x[c] = block
    tables = (pltpu.with_memory_space_constraint(grad_out, pltpu.HBM), out_other)
    r = list(place("place_scaled", plan, where, metas, tables, cap, True, list(range(len(x)))))
    placings = (placing, placing_other)

    def over(blocks, which):
        for c in which:
            blocks[c] = swap(blocks[c], "expert", 2 * c)

    def share(blocks):
        return [swap(jnp.concatenate([blocks[c] for c in plan.far], axis=0), "dp", 1)]

    def pick(blocks, which):
        return [blocks[c] for c in which]

    over(x, plan.far)
    over(r, plan.far)
    x_others, r_others = share(x), share(r)
    over(x, plan.near)
    for c in plan.near:
        r[c] = after(r[c], *x_others)
    over(r, plan.near)

    x_all, hidden, to_a, to_b = forward(
        "forward_own_and_far", where, 0, pick(x, [0]), pick(x, plan.far), x_others, w_gate, w_up
    )
    r_all, grad_a, grad_b = backward(
        "backward_own_and_far", where, 0, pick(r, [0]), pick(r, plan.far), r_others, w_down, to_a, to_b
    )
    own, give, keep = first_grad(plan, where, grad_a, grad_b, w_gate, w_up, dp, cap)
    got = swap(give, "dp", 1)

    x_all, hidden, to_a, to_b = forward(
        "forward_near", where, 1, pick(x, plan.near), [], [], w_gate, w_up, (after(x_all, give), hidden)
    )
    far_sum = (keep + after(got, hidden, *pick(r, plan.near)).astype(F32)).astype(BF16)
    rows = 2 * cap
    far = [swap(far_sum[i * rows : (i + 1) * rows], "expert", 2 * c) for i, c in enumerate(plan.far)]
    kept = (after(r_all, far_sum), after(grad_a, give), after(grad_b, give))
    r_all, grad_a, grad_b = backward(
        "backward_near", where, 1, pick(r, plan.near), [], [], w_down, to_a, to_b, kept
    )
    away_part = near_grad(plan, where, grad_a, grad_b, w_gate, w_up, dp, cap, True)
    grad_a = after(grad_a, away_part[0], *(far if FAR_FIRST == "here" else []))
    here_part = near_grad(plan, where, grad_a, grad_b, w_gate, w_up, dp, cap, False)

    def send_back(part):
        return [swap(b, "expert", 2 * c) for b, c in zip(part, plan.near, strict=True)]

    away_rows, here_rows = send_back(away_part), send_back(here_part)
    slab = width // dp
    away, here = list(range(dp // 2, dp)), list(range(dp // 2))

    hidden = after(hidden, here_part[0], *(far if FAR_FIRST == "down" else []))
    (grad_down,) = outer("down_grad", where, hidden, [r_all])
    away_rows[0] = after(away_rows[0], grad_down)
    away_sum, other = combine(
        plan, where, placings, [own, *far, *away_rows], dp, cap, away, True
    )
    other = swap(other, "expert", 1)
    away_sum = (away_sum + other.astype(F32)).astype(BF16)
    parts = [away_sum[:, n * slab : (n + 1) * slab] for n in range(len(away))]
    away_sums = [swap(part, "dp", s) for part, s in zip(parts, away, strict=True)]
    rights = [grad_a, grad_b]
    x_all = after(x_all, *parts)
    early = 1 if LATE_QUARTER else 2
    grads = ()
    for part in range(early):
        grads = outer(f"gate_and_up_{part}", where, x_all, rights, part, 4, grads)
    here_rows[0] = after(here_rows[0], grads[0])
    total, other, *rest = combine(
        plan, where, placings, [own, *far, *here_rows], dp, cap, here, False
    )
    got = [swap(other, "expert", 1)]
    x_all = after(x_all, total)
    for part in range(early, 4):
        grads = outer(f"gate_and_up_{part}", where, x_all, rights, part, 4, grads)
        for n, s in enumerate(here[1:] if part == early else []):
            if SIDE_LAST == "cross":
                got += [swap(rest[2 * n], "dp", s), cross(rest[2 * n + 1], s)]
            else:
                other = after(swap(rest[2 * n + 1], "expert", 1), grads[0])
                both = rest[2 * n].astype(F32) + other.astype(F32)
                got += [swap(both.astype(BF16), "dp", s)]
    grad_gate, grad_up = grads
    total = total + add_up(away_sums)
    for part in got:
        total = total + part.astype(F32)
    return (total.astype(BF16), grad_gate, grad_up, grad_down)


def solution(mesh):
    in_specs = (
        P("expert", None),
        P("expert", None),
        P("expert", None),
        P("expert", None),
        P("expert", None, "dp"),
        P("expert", None, "dp"),
        P("expert", "dp", None),
    )
    out_specs = (
        P("expert", "dp"),
        P("expert", None, "dp"),
        P("expert", None, "dp"),
        P("expert", "dp", None),
    )
    return jax.shard_map(body, mesh=mesh, in_specs=in_specs, out_specs=out_specs, check_vma=False)
```

```python
import functools

import jax
import jax.numpy as jnp
from jax import lax
from jax.experimental import pallas as pl
from jax.experimental.pallas import tpu as pltpu
from jax.sharding import PartitionSpec as P

F32 = jnp.float32
BF16 = jnp.bfloat16
VMEM_LIMIT = 20 * 1024 * 1024
COST = {"forward_near": 60000, "backward_near": 1000, "own_and_far_input_grads": 100, "near_grads_away": 20000, "near_grads_here": 100, "gate_and_up_0": 1000, "gate_and_up_1": 5000, "gate_and_up_2": 20000, "gate_and_up_3": 20000, "combine_away": 20000, "combine_here": 20000, "place_tokens": 100}
COST = {name: 10**6 * cost for name, cost in COST.items()}
FAR_FIRST = 'down'
SIDE_LAST = 'core'
OPT_DOWN_LATE = True
OPT_FAR_WAITS = False


def contract(left, right, left_dim, right_dim):
    return lax.dot_general(
        left, right, (((left_dim,), (right_dim,)), ((), ())), preferred_element_type=F32
    )


def like(*shape, dtype=BF16):
    return jax.ShapeDtypeStruct(shape, dtype)


def estimate(name):
    return pl.CostEstimate(flops=COST.get(name, 0), bytes_accessed=0, transcendentals=0)


def call(kernel, name, where, args, in_specs, out_shape, out_specs, grid, kept=()):
    args = (*kept, *args)
    in_specs = [pl.BlockSpec(memory_space=pl.ANY)] * len(kept) + in_specs

    def inner(where, *refs):
        kernel(where, *refs[len(kept) :])

    return pl.pallas_call(
        inner,
        input_output_aliases={i + 1: i for i in range(len(kept))},
        grid_spec=pltpu.PrefetchScalarGridSpec(
            num_scalar_prefetch=1, grid=grid, in_specs=in_specs, out_specs=out_specs
        ),
        out_shape=out_shape,
        name=name,
        compiler_params=pltpu.CompilerParams(vmem_limit_bytes=VMEM_LIMIT),
        cost_estimate=estimate(name),
    )(where, *args)


def whole(array):
    return pl.BlockSpec(array.shape, lambda *_: (0,) * len(array.shape))


class Plan:
    def __init__(self, experts):
        chips = experts // 2
        by_hops = sorted(range(1, chips), key=lambda c: (-c.bit_count(), c))
        self.experts = experts
        self.far = sorted(by_hops[: chips // 2 - 1])
        self.near = sorted(by_hops[chips // 2 - 1 :])
        self.chips = [0] + self.far + self.near


def after(array, *earlier):
    return lax.optimization_barrier((array, *earlier))[0]


def place_kernel(plan, cap, with_gate, chips, placings, where, *refs):
    metas, tables, outs = refs[:2], refs[2:4], refs[4:]
    experts = plan.experts
    toks, width = tables[0].shape
    half = pl.ds(pl.multiple_of((where[1] & 1) * (width // 2), 128), width // 2)
    earlier = (
        lax.broadcasted_iota(jnp.int32, (toks, toks), 0)
        < lax.broadcasted_iota(jnp.int32, (toks, toks), 1)
    ).astype(BF16)
    slot = lax.broadcasted_iota(jnp.int32, (cap, toks), 0)
    for side in range(2):
        ids = metas[side][0:2, :].astype(jnp.int32) ^ where[0]
        ids0, ids1 = ids[0:1, :], ids[1:2, :]
        rel = lax.broadcasted_iota(jnp.int32, (experts, toks), 0)
        match = (rel == ids0) | (rel == ids1)
        rank = jnp.dot(match.astype(BF16), earlier, preferred_element_type=F32).astype(jnp.int32)
        rank = jnp.where(match, rank, -1)
        for place, chip in enumerate(plan.chips):
            d = 2 * chip
            placing = slot == rank[d : d + 1, :]
            if placings:
                outs[len(chips) + side][place * cap : (place + 1) * cap, :] = placing.astype(BF16)
            if chip not in chips:
                continue
            rows = tables[side][:, half] if chip in plan.far else tables[side][...]
            block = jnp.dot(placing.astype(BF16), rows, preferred_element_type=F32)
            if with_gate:
                gate = jnp.where(ids0 == d, metas[side][2:3, :], metas[side][3:4, :])
                slot_gate = jnp.sum(jnp.where(placing, gate, 0.0), axis=1, keepdims=True)
                block = block * slot_gate
            outs[chips.index(chip)][side * cap : (side + 1) * cap, :] = block.astype(BF16)


def place(name, plan, where, metas, tables, cap, with_gate, chips, placings=False):
    toks, width = tables[0].shape
    outs = [like(2 * cap, width // 2 if c in plan.far else width) for c in chips]
    if placings:
        outs = outs + [like(len(plan.chips) * cap, toks)] * 2
    args = (*metas, *tables)
    return call(
        functools.partial(place_kernel, plan, cap, with_gate, chips, placings),
        name,
        where,
        args,
        [whole(a) for a in args],
        outs,
        [whole(o) for o in outs],
        (1,),
    )


def gather_blocks(where, out_ref, full, halves, others):
    cap = full[0].shape[0]
    width = out_ref.shape[1]
    part = width // 2
    for i, block in enumerate(full):
        out_ref[i * cap : (i + 1) * cap, :] = block[...]
    if not halves:
        return
    mine = pl.ds(pl.multiple_of((where[1] & 1) * part, 128), part)
    theirs = pl.ds(pl.multiple_of((1 - (where[1] & 1)) * part, 128), part)
    base = len(full) * cap
    for i, block in enumerate(halves):
        out_ref[base + i * cap : base + (i + 1) * cap, mine] = block[...]
    out_ref[base : base + len(halves) * cap, theirs] = others[...]


def split_refs(refs, n_full, n_halves):
    full = refs[:n_full]
    halves = refs[n_full : n_full + n_halves]
    rest = refs[n_full + n_halves :]
    if n_halves:
        return full, halves, rest[0], rest[1:]
    return full, halves, None, rest


def forward_kernel(n_full, n_halves, where, *refs):
    full, halves, others, rest = split_refs(refs, n_full, n_halves)
    gate_ref, up_ref, rows_ref, hidden_ref, to_a_ref, to_b_ref = rest

    @pl.when(pl.program_id(0) == 0)
    def _():
        gather_blocks(where, rows_ref, full, halves, others)

    rows = rows_ref[...]
    pre_gate = jnp.dot(rows, gate_ref[0], preferred_element_type=F32)
    pre_up = jnp.dot(rows, up_ref[0], preferred_element_type=F32)
    squash = jax.nn.sigmoid(pre_gate)
    swish = squash * pre_gate
    hidden_ref[...] = (swish * pre_up).astype(BF16)
    to_a_ref[...] = pre_up * squash * (1.0 + pre_gate * (1.0 - squash))
    to_b_ref[...] = swish


def forward(name, where, chunk, full, halves, others, w_gate, w_up, kept=()):
    cap, width = full[0].shape
    count = (len(full) + len(halves)) * cap
    rows = 2 * count
    units = w_gate.shape[2]
    tile = 256
    blocks = [*full, *halves, *others]
    column = pl.BlockSpec((1, width, tile), lambda j, _: (0, 0, j))
    out_column = pl.BlockSpec((count, tile), lambda j, _: (0, j))
    outs = [
        like(rows, width),
        like(rows, units),
        like(count, units, dtype=F32),
        like(count, units, dtype=F32),
    ]
    return call(
        functools.partial(forward_kernel, len(full), len(halves)),
        name,
        where,
        (*blocks, w_gate, w_up),
        [whole(b) for b in blocks] + [column, column],
        outs,
        [
            pl.BlockSpec((count, width), lambda j, _: (chunk, 0)),
            pl.BlockSpec((count, tile), lambda j, _: (chunk, j)),
            out_column,
            out_column,
        ],
        (units // tile,),
        kept,
    )


def backward_kernel(n_full, n_halves, where, *refs):
    full, halves, others, rest = split_refs(refs, n_full, n_halves)
    down_ref, to_a_ref, to_b_ref, rows_ref, grad_a_ref, grad_b_ref = rest

    @pl.when(pl.program_id(0) == 0)
    def _():
        gather_blocks(where, rows_ref, full, halves, others)

    grad_hidden = contract(rows_ref[...], down_ref[0], 1, 1)
    grad_a_ref[...] = (grad_hidden * to_a_ref[...]).astype(BF16)
    grad_b_ref[...] = (grad_hidden * to_b_ref[...]).astype(BF16)


def backward(name, where, chunk, full, halves, others, w_down, to_a, to_b, kept=()):
    cap, width = full[0].shape
    count = (len(full) + len(halves)) * cap
    rows = 2 * count
    units = w_down.shape[1]
    tile = 256
    blocks = [*full, *halves, *others]
    column = pl.BlockSpec((count, tile), lambda j, _: (0, j))
    out_column = pl.BlockSpec((count, tile), lambda j, _: (chunk, j))
    outs = [like(rows, width), like(rows, units), like(rows, units)]
    return call(
        functools.partial(backward_kernel, len(full), len(halves)),
        name,
        where,
        (*blocks, w_down, to_a, to_b),
        [whole(b) for b in blocks]
        + [pl.BlockSpec((1, tile, width), lambda j, _: (0, j, 0)), column, column],
        outs,
        [pl.BlockSpec((count, width), lambda j, _: (chunk, 0)), out_column, out_column],
        (units // tile,),
        kept,
    )


def input_grad(grad_a_ref, grad_b_ref, gate_ref, up_ref):
    return contract(grad_a_ref[...], gate_ref[0], 1, 1) + contract(
        grad_b_ref[...], up_ref[0], 1, 1
    )


def first_grad_kernel(cap, where, grad_a_ref, grad_b_ref, gate_ref, up_ref, *outs):
    own_ref, give_ref, keep_ref = outs
    part = input_grad(grad_a_ref, grad_b_ref, gate_ref, up_ref)
    own_ref[...] = part[: 2 * cap].astype(BF16)
    far = part[2 * cap :]
    step, steps = pl.program_id(0), pl.num_programs(0)

    @pl.when(step < steps // 2)
    def _():
        give_ref[...] = far.astype(BF16)

    @pl.when(step >= steps // 2)
    def _():
        keep_ref[...] = far


def first_grad(plan, where, grad_a, grad_b, w_gate, w_up, dp, cap):
    width, units = w_gate.shape[1:]
    slab = width // dp
    far = 2 * len(plan.far) * cap

    def at(i, where):
        parity = where[1] & 1
        late = jnp.where(i < dp // 2, 1 - parity, parity)
        return 2 * lax.rem(i, dp // 2) + late

    weight = pl.BlockSpec((1, slab, units), lambda i, where: (0, at(i, where), 0))
    chunk = pl.BlockSpec((grad_a.shape[0] // 2, units), lambda i, where: (0, 0))
    outs = [
        like(2 * cap, width),
        like(far, width // 2),
        like(far, width // 2, dtype=F32),
    ]
    return call(
        functools.partial(first_grad_kernel, cap),
        "own_and_far_input_grads",
        where,
        (grad_a, grad_b, w_gate, w_up),
        [chunk, chunk, weight, weight],
        outs,
        [
            pl.BlockSpec((2 * cap, slab), lambda i, where: (0, at(i, where))),
            pl.BlockSpec((far, slab), lambda i, where: (0, jnp.minimum(i, dp // 2 - 1))),
            pl.BlockSpec((far, slab), lambda i, where: (0, jnp.maximum(i - dp // 2, 0))),
        ],
        (dp,),
    )


def near_grad_kernel(cap, where, grad_a_ref, grad_b_ref, gate_ref, up_ref, *outs):
    part = input_grad(grad_a_ref, grad_b_ref, gate_ref, up_ref)
    for i, out in enumerate(outs):
        out[...] = part[2 * i * cap : 2 * (i + 1) * cap].astype(BF16)


def near_grad(plan, where, grad_a, grad_b, w_gate, w_up, dp, cap, away):
    width, units = w_gate.shape[1:]
    tile = width // 4
    steps = 2

    def at(i, where):
        side = (where[1] >= dp // 2).astype(jnp.int32)
        return steps * (1 - side if away else side) + i

    weight = pl.BlockSpec((1, tile, units), lambda i, where: (0, at(i, where), 0))
    chunk = pl.BlockSpec((grad_a.shape[0] // 2, units), lambda i, where: (1, 0))
    outs = [like(2 * cap, width // 2)] * len(plan.near)
    return call(
        functools.partial(near_grad_kernel, cap),
        "near_grads_away" if away else "near_grads_here",
        where,
        (grad_a, grad_b, w_gate, w_up),
        [chunk, chunk, weight, weight],
        outs,
        [pl.BlockSpec((2 * cap, tile), lambda i, where: (0, i))] * len(plan.near),
        (steps,),
    )


def outer_kernel(n_right, where, left_ref, *refs):
    left = left_ref[...].T
    for right, out in zip(refs[:n_right], refs[n_right:], strict=True):
        out[0] = jnp.dot(left, right[...], preferred_element_type=F32).astype(BF16)


def outer(name, where, left, rights, part=0, parts=1, kept=()):
    rows, width = left.shape
    tile = 256
    steps = width // tile // parts
    first = part * steps
    outs = [like(1, width, r.shape[1]) for r in rights]
    return call(
        functools.partial(outer_kernel, len(rights)),
        name,
        where,
        (left, *rights),
        [pl.BlockSpec((rows, tile), lambda i, _: (0, first + i))] + [whole(r) for r in rights],
        outs,
        [pl.BlockSpec((1, tile, o.shape[2]), lambda i, _: (0, first + i, 0)) for o in outs],
        (steps,),
        kept,
    )


def combine_kernel(plan, cap, dp, shifts, side_by_side, where, *refs):
    chips = len(plan.chips)
    placings, blocks, outs, rows_ref = refs[:2], refs[2 : 2 + chips], refs[2 + chips : -1], refs[-1]
    slab = rows_ref.shape[1]
    side_rows = chips * cap
    for n, shift in enumerate(shifts):
        to = where[1] ^ shift
        for place, (chip, block) in enumerate(zip(plan.chips, blocks, strict=True)):
            if chip == 0:
                column = to
            elif chip in plan.far:
                column = to >> 1
            else:
                column = lax.rem(to, dp // 2)
            column = pl.ds(pl.multiple_of(column * slab, 128), slab)
            for side in range(2):
                base = side * side_rows + place * cap
                if chip in plan.far and shift % 2:
                    rows_ref[base : base + cap, :] = jnp.zeros((cap, slab), BF16)
                else:
                    rows_ref[base : base + cap, :] = block[side * cap : (side + 1) * cap, column]
        own = contract(placings[0][...], rows_ref[:side_rows, :], 0, 0)
        other = contract(placings[1][...], rows_ref[side_rows:, :], 0, 0)
        if side_by_side:
            outs[0][:, n * slab : (n + 1) * slab] = own
            outs[1][:, n * slab : (n + 1) * slab] = other.astype(BF16)
        else:
            outs[2 * n][...] = own.astype(outs[2 * n].dtype)
            outs[2 * n + 1][...] = other.astype(BF16)


def combine(plan, where, placings, blocks, dp, cap, shifts, side_by_side):
    width = blocks[0].shape[1]
    slab = width // dp
    toks = placings[0].shape[1]
    args = (*placings, *blocks)
    if side_by_side:
        outs = [like(toks, slab * len(shifts), dtype=F32), like(toks, slab * len(shifts))]
    else:
        pairs = [[like(toks, slab, dtype=BF16 if s else F32), like(toks, slab)] for s in shifts]
        outs = [o for pair in pairs for o in pair]
    moved = sum(a.size * a.dtype.itemsize for a in args)
    flops = 4 * placings[0].size * slab * len(shifts)
    return pl.pallas_call(
        functools.partial(combine_kernel, plan, cap, dp, shifts, side_by_side),
        grid_spec=pltpu.PrefetchScalarGridSpec(
            num_scalar_prefetch=1,
            grid=(1,),
            in_specs=[whole(a) for a in args],
            out_specs=[whole(o) for o in outs],
            scratch_shapes=[pltpu.VMEM((plan.experts * cap, slab), BF16)],
        ),
        out_shape=outs,
        name="combine_away" if side_by_side else "combine_here",
        compiler_params=pltpu.CompilerParams(vmem_limit_bytes=VMEM_LIMIT),
        cost_estimate=pl.CostEstimate(
            flops=0, bytes_accessed=0, transcendentals=0
        ),
    )(where, *args)


def sum_kernel(*refs):
    *parts, out = refs
    out[...] = functools.reduce(lambda a, b: a + b, [p[...].astype(F32) for p in parts])


def add_up(parts):
    out = like(*parts[0].shape, dtype=F32)
    return pl.pallas_call(
        sum_kernel,
        out_shape=out,
        name="add_up",
        compiler_params=pltpu.CompilerParams(vmem_limit_bytes=VMEM_LIMIT),
        cost_estimate=estimate("add_up"),
    )(*parts)


def swap(rows, axis, mask):
    count = lax.axis_size(axis)
    return lax.ppermute(rows, axis, [(i, i ^ mask) for i in range(count)])


def cross(rows, shift):
    dp = lax.axis_size("dp")
    count = lax.axis_size("expert") * dp
    return lax.ppermute(rows, ("expert", "dp"), [(i, i ^ (dp + shift)) for i in range(count)])


def body(tokens, grad_out, expert_ids, gate_vals, w_gate, w_up, w_down):
    plan = Plan(lax.axis_size("expert"))
    dp = lax.axis_size("dp")
    toks, width = tokens.shape
    cap = 3 * toks // plan.experts
    where = jnp.stack([lax.axis_index("expert"), lax.axis_index("dp")]).astype(jnp.int32)
    meta = jnp.concatenate([expert_ids.T.astype(F32), gate_vals.T], axis=0)
    meta_other = swap(meta, "expert", 1)
    tokens_other = swap(tokens, "expert", 1)
    out_other = swap(grad_out, "expert", 1)
    metas = (meta, meta_other)
    tables = (pltpu.with_memory_space_constraint(tokens, pltpu.HBM), tokens_other)
    x = [None] * len(plan.chips)
    blocks = place("place_far_tokens", plan, where, metas, tables, cap, False, plan.far)
    for c, block in zip(plan.far, blocks, strict=True):
        x[c] = block
    rest = [0] + plan.near
    metas = (after(meta, x[plan.far[-1]]), meta_other)
    *blocks, placing, placing_other = place(
        "place_tokens", plan, where, metas, tables, cap, False, rest, True
    )
    for c, block in zip(rest, blocks, strict=True):
        x[c] = block
    tables = (pltpu.with_memory_space_constraint(grad_out, pltpu.HBM), out_other)
    r = list(place("place_scaled", plan, where, metas, tables, cap, True, list(range(len(x)))))
    placings = (placing, placing_other)

    def over(blocks, which):
        for c in which:
            blocks[c] = swap(blocks[c], "expert", 2 * c)

    def share(blocks):
        return [swap(jnp.concatenate([blocks[c] for c in plan.far], axis=0), "dp", 1)]

    def pick(blocks, which):
        return [blocks[c] for c in which]

    over(x, plan.far)
    over(r, plan.far)
    x_others, r_others = share(x), share(r)
    over(x, plan.near)
    for c in plan.near:
        r[c] = after(r[c], *x_others)
    over(r, plan.near)

    x_all, hidden, to_a, to_b = forward(
        "forward_own_and_far", where, 0, pick(x, [0]), pick(x, plan.far), x_others, w_gate, w_up
    )
    r_all, grad_a, grad_b = backward(
        "backward_own_and_far", where, 0, pick(r, [0]), pick(r, plan.far), r_others, w_down, to_a, to_b
    )
    own, give, keep = first_grad(plan, where, grad_a, grad_b, w_gate, w_up, dp, cap)
    got = swap(give, "dp", 1)

    x_all, hidden, to_a, to_b = forward(
        "forward_near", where, 1, pick(x, plan.near), [], [], w_gate, w_up, (after(x_all, give), hidden)
    )
    far_sum = (keep + after(got, hidden, *(pick(r, plan.near) if OPT_FAR_WAITS else [])).astype(F32)).astype(BF16)
    rows = 2 * cap
    far = [swap(far_sum[i * rows : (i + 1) * rows], "expert", 2 * c) for i, c in enumerate(plan.far)]
    kept = (after(r_all, far_sum), after(grad_a, give), after(grad_b, give))
    r_all, grad_a, grad_b = backward(
        "backward_near", where, 1, pick(r, plan.near), [], [], w_down, to_a, to_b, kept
    )
    away_part = near_grad(plan, where, grad_a, grad_b, w_gate, w_up, dp, cap, True)
    grad_a = after(grad_a, away_part[0], *(far if FAR_FIRST == "here" else []))
    here_part = near_grad(plan, where, grad_a, grad_b, w_gate, w_up, dp, cap, False)

    def send_back(part):
        return [swap(b, "expert", 2 * c) for b, c in zip(part, plan.near, strict=True)]

    away_rows, here_rows = send_back(away_part), send_back(here_part)
    slab = width // dp
    away, here = list(range(dp // 2, dp)), list(range(dp // 2))

    rights = [grad_a, grad_b]
    first = [here_part[0], *(far if FAR_FIRST == "down" else [])]
    if OPT_DOWN_LATE:
        grads = outer("gate_and_up_0", where, after(x_all, *first), rights, 0, 4)
        away_rows[0] = after(away_rows[0], grads[0])
    else:
        (grad_down,) = outer("down_grad", where, after(hidden, *first), [r_all])
        away_rows[0] = after(away_rows[0], grad_down)
    away_sum, other = combine(
        plan, where, placings, [own, *far, *away_rows], dp, cap, away, True
    )
    other = swap(other, "expert", 1)
    away_sum = (away_sum + other.astype(F32)).astype(BF16)
    parts = [away_sum[:, n * slab : (n + 1) * slab] for n in range(len(away))]
    away_sums = [swap(part, "dp", s) for part, s in zip(parts, away, strict=True)]
    if OPT_DOWN_LATE:
        (grad_down,) = outer("down_grad", where, after(hidden, *parts), [r_all])
        here_rows[0] = after(here_rows[0], grad_down)
    else:
        grads = outer("gate_and_up_0", where, after(x_all, *parts), rights, 0, 4)
        here_rows[0] = after(here_rows[0], grads[0])
    total, other, *rest = combine(
        plan, where, placings, [own, *far, *here_rows], dp, cap, here, False
    )
    got = [swap(other, "expert", 1)]
    x_all = after(x_all, total)
    for part in range(1, 4):
        grads = outer(f"gate_and_up_{part}", where, x_all, rights, part, 4, grads)
        for n, s in enumerate(here[1:] if part == 1 else []):
            if SIDE_LAST == "cross":
                got += [swap(rest[2 * n], "dp", s), cross(rest[2 * n + 1], s)]
            else:
                other = after(swap(rest[2 * n + 1], "expert", 1), grads[0])
                both = rest[2 * n].astype(F32) + other.astype(F32)
                got += [swap(both.astype(BF16), "dp", s)]
    grad_gate, grad_up = grads
    total = total + add_up(away_sums)
    for part in got:
        total = total + part.astype(F32)
    return (total.astype(BF16), grad_gate, grad_up, grad_down)


def solution(mesh):
    in_specs = (
        P("expert", None),
        P("expert", None),
        P("expert", None),
        P("expert", None),
        P("expert", None, "dp"),
        P("expert", None, "dp"),
        P("expert", "dp", None),
    )
    out_specs = (
        P("expert", "dp"),
        P("expert", None, "dp"),
        P("expert", None, "dp"),
        P("expert", "dp", None),
    )
    return jax.shard_map(body, mesh=mesh, in_specs=in_specs, out_specs=out_specs, check_vma=False)
```

```python
import functools

import jax
import jax.numpy as jnp
from jax import lax
from jax.experimental import pallas as pl
from jax.experimental.pallas import tpu as pltpu
from jax.sharding import PartitionSpec as P

F32 = jnp.float32
BF16 = jnp.bfloat16
VMEM_LIMIT = 20 * 1024 * 1024
COST = {"forward_near": 60000, "backward_near": 1000, "own_and_far_input_grads": 100, "near_grads_away": 20000, "near_grads_here": 100, "gate_and_up_0": 1000, "gate_and_up_1": 5000, "gate_and_up_2": 20000, "gate_and_up_3": 20000, "combine_away": 20000, "combine_here": 20000, "place_tokens": 100}
COST = {name: 10**6 * cost for name, cost in COST.items()}


def contract(left, right, left_dim, right_dim):
    return lax.dot_general(
        left, right, (((left_dim,), (right_dim,)), ((), ())), preferred_element_type=F32
    )


def like(*shape, dtype=BF16):
    return jax.ShapeDtypeStruct(shape, dtype)


def estimate(name):
    return pl.CostEstimate(flops=COST.get(name, 0), bytes_accessed=0, transcendentals=0)


def call(kernel, name, where, args, in_specs, out_shape, out_specs, grid, kept=()):
    args = (*kept, *args)
    in_specs = [pl.BlockSpec(memory_space=pl.ANY)] * len(kept) + in_specs

    def inner(where, *refs):
        kernel(where, *refs[len(kept) :])

    return pl.pallas_call(
        inner,
        input_output_aliases={i + 1: i for i in range(len(kept))},
        grid_spec=pltpu.PrefetchScalarGridSpec(
            num_scalar_prefetch=1, grid=grid, in_specs=in_specs, out_specs=out_specs
        ),
        out_shape=out_shape,
        name=name,
        compiler_params=pltpu.CompilerParams(vmem_limit_bytes=VMEM_LIMIT),
        cost_estimate=estimate(name),
    )(where, *args)


def whole(array):
    return pl.BlockSpec(array.shape, lambda *_: (0,) * len(array.shape))


class Plan:
    def __init__(self, experts):
        chips = experts // 2
        by_hops = sorted(range(1, chips), key=lambda c: (-c.bit_count(), c))
        self.experts = experts
        self.far = sorted(by_hops[: chips // 2 - 1])
        self.near = sorted(by_hops[chips // 2 - 1 :])
        self.chips = [0] + self.far + self.near


def after(array, *earlier):
    return lax.optimization_barrier((array, *earlier))[0]


def place_kernel(plan, cap, with_gate, chips, placings, where, *refs):
    metas, tables, outs = refs[:2], refs[2:4], refs[4:]
    experts = plan.experts
    toks, width = tables[0].shape
    half = pl.ds(pl.multiple_of((where[1] & 1) * (width // 2), 128), width // 2)
    earlier = (
        lax.broadcasted_iota(jnp.int32, (toks, toks), 0)
        < lax.broadcasted_iota(jnp.int32, (toks, toks), 1)
    ).astype(BF16)
    slot = lax.broadcasted_iota(jnp.int32, (cap, toks), 0)
    for side in range(2):
        ids = metas[side][0:2, :].astype(jnp.int32) ^ where[0]
        ids0, ids1 = ids[0:1, :], ids[1:2, :]
        rel = lax.broadcasted_iota(jnp.int32, (experts, toks), 0)
        match = (rel == ids0) | (rel == ids1)
        rank = jnp.dot(match.astype(BF16), earlier, preferred_element_type=F32).astype(jnp.int32)
        rank = jnp.where(match, rank, -1)
        for place, chip in enumerate(plan.chips):
            d = 2 * chip
            placing = slot == rank[d : d + 1, :]
            if placings:
                outs[len(chips) + side][place * cap : (place + 1) * cap, :] = placing.astype(BF16)
            if chip not in chips:
                continue
            narrow = chip in plan.far and width > outs[chips.index(chip)].shape[1]
            rows = tables[side][:, half] if narrow else tables[side][...]
            block = jnp.dot(placing.astype(BF16), rows, preferred_element_type=F32)
            if with_gate:
                gate = jnp.where(ids0 == d, metas[side][2:3, :], metas[side][3:4, :])
                slot_gate = jnp.sum(jnp.where(placing, gate, 0.0), axis=1, keepdims=True)
                block = block * slot_gate
            outs[chips.index(chip)][side * cap : (side + 1) * cap, :] = block.astype(BF16)


def place(name, plan, where, metas, tables, cap, with_gate, chips, placings=False):
    toks, width = tables[0].shape
    outs = [like(2 * cap, width // 2 if c in plan.far else width) for c in chips]
    if placings:
        outs = outs + [like(len(plan.chips) * cap, toks)] * 2
    args = (*metas, *tables)
    specs = [whole(a) for a in args]
    if chips == plan.far:
        half = pl.BlockSpec((toks, width // 2), lambda i, where: (0, where[1] & 1))
        specs = specs[:2] + [half, half]
    return call(
        functools.partial(place_kernel, plan, cap, with_gate, chips, placings),
        name,
        where,
        args,
        specs,
        outs,
        [whole(o) for o in outs],
        (1,),
    )


def gather_blocks(where, out_ref, full, halves, others):
    cap = full[0].shape[0]
    width = out_ref.shape[1]
    part = width // 2
    for i, block in enumerate(full):
        out_ref[i * cap : (i + 1) * cap, :] = block[...]
    if not halves:
        return
    mine = pl.ds(pl.multiple_of((where[1] & 1) * part, 128), part)
    theirs = pl.ds(pl.multiple_of((1 - (where[1] & 1)) * part, 128), part)
    base = len(full) * cap
    for i, block in enumerate(halves):
        out_ref[base + i * cap : base + (i + 1) * cap, mine] = block[...]
    out_ref[base : base + len(halves) * cap, theirs] = others[...]


def split_refs(refs, n_full, n_halves):
    full = refs[:n_full]
    halves = refs[n_full : n_full + n_halves]
    rest = refs[n_full + n_halves :]
    if n_halves:
        return full, halves, rest[0], rest[1:]
    return full, halves, None, rest


def forward_kernel(n_full, n_halves, where, *refs):
    full, halves, others, rest = split_refs(refs, n_full, n_halves)
    gate_ref, up_ref, rows_ref, hidden_ref, to_a_ref, to_b_ref = rest

    @pl.when(pl.program_id(0) == 0)
    def _():
        gather_blocks(where, rows_ref, full, halves, others)

    rows = rows_ref[...]
    pre_gate = jnp.dot(rows, gate_ref[0], preferred_element_type=F32)
    pre_up = jnp.dot(rows, up_ref[0], preferred_element_type=F32)
    squash = jax.nn.sigmoid(pre_gate)
    swish = squash * pre_gate
    hidden_ref[...] = (swish * pre_up).astype(BF16)
    to_a_ref[...] = pre_up * squash * (1.0 + pre_gate * (1.0 - squash))
    to_b_ref[...] = swish


def forward(name, where, chunk, full, halves, others, w_gate, w_up, kept=()):
    cap, width = full[0].shape
    count = (len(full) + len(halves)) * cap
    rows = 2 * count
    units = w_gate.shape[2]
    tile = 256
    blocks = [*full, *halves, *others]
    column = pl.BlockSpec((1, width, tile), lambda j, _: (0, 0, j))
    out_column = pl.BlockSpec((count, tile), lambda j, _: (0, j))
    outs = [
        like(rows, width),
        like(rows, units),
        like(count, units, dtype=F32),
        like(count, units, dtype=F32),
    ]
    return call(
        functools.partial(forward_kernel, len(full), len(halves)),
        name,
        where,
        (*blocks, w_gate, w_up),
        [whole(b) for b in blocks] + [column, column],
        outs,
        [
            pl.BlockSpec((count, width), lambda j, _: (chunk, 0)),
            pl.BlockSpec((count, tile), lambda j, _: (chunk, j)),
            out_column,
            out_column,
        ],
        (units // tile,),
        kept,
    )


def backward_kernel(n_full, n_halves, where, *refs):
    full, halves, others, rest = split_refs(refs, n_full, n_halves)
    down_ref, to_a_ref, to_b_ref, rows_ref, grad_a_ref, grad_b_ref = rest

    @pl.when(pl.program_id(0) == 0)
    def _():
        gather_blocks(where, rows_ref, full, halves, others)

    grad_hidden = contract(rows_ref[...], down_ref[0], 1, 1)
    grad_a_ref[...] = (grad_hidden * to_a_ref[...]).astype(BF16)
    grad_b_ref[...] = (grad_hidden * to_b_ref[...]).astype(BF16)


def backward(name, where, chunk, full, halves, others, w_down, to_a, to_b, kept=()):
    cap, width = full[0].shape
    count = (len(full) + len(halves)) * cap
    rows = 2 * count
    units = w_down.shape[1]
    tile = 512
    blocks = [*full, *halves, *others]
    column = pl.BlockSpec((count, tile), lambda j, _: (0, j))
    out_column = pl.BlockSpec((count, tile), lambda j, _: (chunk, j))
    outs = [like(rows, width), like(rows, units), like(rows, units)]
    return call(
        functools.partial(backward_kernel, len(full), len(halves)),
        name,
        where,
        (*blocks, w_down, to_a, to_b),
        [whole(b) for b in blocks]
        + [pl.BlockSpec((1, tile, width), lambda j, _: (0, j, 0)), column, column],
        outs,
        [pl.BlockSpec((count, width), lambda j, _: (chunk, 0)), out_column, out_column],
        (units // tile,),
        kept,
    )


def input_grad(grad_a_ref, grad_b_ref, gate_ref, up_ref):
    return contract(grad_a_ref[...], gate_ref[0], 1, 1) + contract(
        grad_b_ref[...], up_ref[0], 1, 1
    )


def first_grad_kernel(cap, where, grad_a_ref, grad_b_ref, gate_ref, up_ref, *outs):
    own_ref, give_ref, keep_ref = outs
    part = input_grad(grad_a_ref, grad_b_ref, gate_ref, up_ref)
    own_ref[...] = part[: 2 * cap].astype(BF16)
    far = part[2 * cap :]
    step, steps = pl.program_id(0), pl.num_programs(0)

    @pl.when(step < steps // 2)
    def _():
        give_ref[...] = far.astype(BF16)

    @pl.when(step >= steps // 2)
    def _():
        keep_ref[...] = far


def first_grad(plan, where, grad_a, grad_b, w_gate, w_up, dp, cap):
    width, units = w_gate.shape[1:]
    slab = width // dp
    far = 2 * len(plan.far) * cap

    def at(i, where):
        parity = where[1] & 1
        late = jnp.where(i < dp // 2, 1 - parity, parity)
        return 2 * lax.rem(i, dp // 2) + late

    weight = pl.BlockSpec((1, slab, units), lambda i, where: (0, at(i, where), 0))
    chunk = pl.BlockSpec((grad_a.shape[0] // 2, units), lambda i, where: (0, 0))
    outs = [
        like(2 * cap, width),
        like(far, width // 2),
        like(far, width // 2, dtype=F32),
    ]
    return call(
        functools.partial(first_grad_kernel, cap),
        "own_and_far_input_grads",
        where,
        (grad_a, grad_b, w_gate, w_up),
        [chunk, chunk, weight, weight],
        outs,
        [
            pl.BlockSpec((2 * cap, slab), lambda i, where: (0, at(i, where))),
            pl.BlockSpec((far, slab), lambda i, where: (0, jnp.minimum(i, dp // 2 - 1))),
            pl.BlockSpec((far, slab), lambda i, where: (0, jnp.maximum(i - dp // 2, 0))),
        ],
        (dp,),
    )


def near_grad_kernel(cap, where, grad_a_ref, grad_b_ref, gate_ref, up_ref, *outs):
    part = input_grad(grad_a_ref, grad_b_ref, gate_ref, up_ref)
    for i, out in enumerate(outs):
        out[...] = part[2 * i * cap : 2 * (i + 1) * cap].astype(BF16)


def near_grad(plan, where, grad_a, grad_b, w_gate, w_up, dp, cap, away):
    width, units = w_gate.shape[1:]
    tile = width // 4
    steps = 2

    def at(i, where):
        side = (where[1] >= dp // 2).astype(jnp.int32)
        return steps * (1 - side if away else side) + i

    weight = pl.BlockSpec((1, tile, units), lambda i, where: (0, at(i, where), 0))
    chunk = pl.BlockSpec((grad_a.shape[0] // 2, units), lambda i, where: (1, 0))
    outs = [like(2 * cap, width // 2)] * len(plan.near)
    return call(
        functools.partial(near_grad_kernel, cap),
        "near_grads_away" if away else "near_grads_here",
        where,
        (grad_a, grad_b, w_gate, w_up),
        [chunk, chunk, weight, weight],
        outs,
        [pl.BlockSpec((2 * cap, tile), lambda i, where: (0, i))] * len(plan.near),
        (steps,),
    )


def outer_kernel(n_right, where, left_ref, *refs):
    left = left_ref[...].T
    for right, out in zip(refs[:n_right], refs[n_right:], strict=True):
        out[0] = jnp.dot(left, right[...], preferred_element_type=F32).astype(BF16)


def outer(name, where, left, rights, part=0, parts=1, kept=()):
    rows, width = left.shape
    tile = 512
    steps = width // tile // parts
    first = part * steps
    outs = [like(1, width, r.shape[1]) for r in rights]
    return call(
        functools.partial(outer_kernel, len(rights)),
        name,
        where,
        (left, *rights),
        [pl.BlockSpec((rows, tile), lambda i, _: (0, first + i))] + [whole(r) for r in rights],
        outs,
        [pl.BlockSpec((1, tile, o.shape[2]), lambda i, _: (0, first + i, 0)) for o in outs],
        (steps,),
        kept,
    )


def combine_kernel(plan, cap, dp, shifts, side_by_side, where, *refs):
    chips = len(plan.chips)
    placings, blocks, outs, rows_ref = refs[:2], refs[2 : 2 + chips], refs[2 + chips : -1], refs[-1]
    slab = rows_ref.shape[1]
    side_rows = chips * cap
    for n, shift in enumerate(shifts):
        to = where[1] ^ shift
        for place, (chip, block) in enumerate(zip(plan.chips, blocks, strict=True)):
            if chip == 0:
                column = to
            elif chip in plan.far:
                column = to >> 1
            else:
                column = lax.rem(to, dp // 2)
            column = pl.ds(pl.multiple_of(column * slab, 128), slab)
            for side in range(2):
                base = side * side_rows + place * cap
                if chip in plan.far and shift % 2:
                    rows_ref[base : base + cap, :] = jnp.zeros((cap, slab), BF16)
                else:
                    rows_ref[base : base + cap, :] = block[side * cap : (side + 1) * cap, column]
        own = contract(placings[0][...], rows_ref[:side_rows, :], 0, 0)
        other = contract(placings[1][...], rows_ref[side_rows:, :], 0, 0)
        if side_by_side:
            outs[0][:, n * slab : (n + 1) * slab] = own
            outs[1][:, n * slab : (n + 1) * slab] = other.astype(BF16)
        else:
            outs[2 * n][...] = own.astype(outs[2 * n].dtype)
            outs[2 * n + 1][...] = other.astype(BF16)


def combine(plan, where, placings, blocks, dp, cap, shifts, side_by_side):
    width = blocks[0].shape[1]
    slab = width // dp
    toks = placings[0].shape[1]
    args = (*placings, *blocks)
    if side_by_side:
        outs = [like(toks, slab * len(shifts), dtype=F32), like(toks, slab * len(shifts))]
    else:
        pairs = [[like(toks, slab, dtype=BF16 if s else F32), like(toks, slab)] for s in shifts]
        outs = [o for pair in pairs for o in pair]
    moved = sum(a.size * a.dtype.itemsize for a in args)
    flops = 4 * placings[0].size * slab * len(shifts)
    return pl.pallas_call(
        functools.partial(combine_kernel, plan, cap, dp, shifts, side_by_side),
        grid_spec=pltpu.PrefetchScalarGridSpec(
            num_scalar_prefetch=1,
            grid=(1,),
            in_specs=[whole(a) for a in args],
            out_specs=[whole(o) for o in outs],
            scratch_shapes=[pltpu.VMEM((plan.experts * cap, slab), BF16)],
        ),
        out_shape=outs,
        name="combine_away" if side_by_side else "combine_here",
        compiler_params=pltpu.CompilerParams(vmem_limit_bytes=VMEM_LIMIT),
        cost_estimate=pl.CostEstimate(
            flops=0, bytes_accessed=0, transcendentals=0
        ),
    )(where, *args)


def sum_kernel(*refs):
    *parts, out = refs
    out[...] = functools.reduce(lambda a, b: a + b, [p[...].astype(F32) for p in parts])


def add_up(parts):
    out = like(*parts[0].shape, dtype=F32)
    return pl.pallas_call(
        sum_kernel,
        out_shape=out,
        name="add_up",
        compiler_params=pltpu.CompilerParams(vmem_limit_bytes=VMEM_LIMIT),
        cost_estimate=estimate("add_up"),
    )(*parts)


def swap(rows, axis, mask):
    count = lax.axis_size(axis)
    return lax.ppermute(rows, axis, [(i, i ^ mask) for i in range(count)])


def body(tokens, grad_out, expert_ids, gate_vals, w_gate, w_up, w_down):
    plan = Plan(lax.axis_size("expert"))
    dp = lax.axis_size("dp")
    toks, width = tokens.shape
    cap = 3 * toks // plan.experts
    where = jnp.stack([lax.axis_index("expert"), lax.axis_index("dp")]).astype(jnp.int32)
    meta = jnp.concatenate([expert_ids.T.astype(F32), gate_vals.T], axis=0)
    meta_other = swap(meta, "expert", 1)
    tokens_other = swap(tokens, "expert", 1)
    out_other = swap(grad_out, "expert", 1)
    metas = (meta, meta_other)
    tables = (pltpu.with_memory_space_constraint(tokens, pltpu.HBM), tokens_other)
    x = [None] * len(plan.chips)
    blocks = place("place_far_tokens", plan, where, metas, tables, cap, False, plan.far)
    for c, block in zip(plan.far, blocks, strict=True):
        x[c] = block
    rest = [0] + plan.near
    metas = (after(meta, x[plan.far[-1]]), meta_other)
    *blocks, placing, placing_other = place(
        "place_tokens", plan, where, metas, tables, cap, False, rest, True
    )
    for c, block in zip(rest, blocks, strict=True):
        x[c] = block
    tables = (pltpu.with_memory_space_constraint(grad_out, pltpu.HBM), out_other)
    r = list(place("place_scaled", plan, where, metas, tables, cap, True, list(range(len(x)))))
    placings = (placing, placing_other)

    def over(blocks, which):
        for c in which:
            blocks[c] = swap(blocks[c], "expert", 2 * c)

    def share(blocks):
        return [swap(jnp.concatenate([blocks[c] for c in plan.far], axis=0), "dp", 1)]

    def pick(blocks, which):
        return [blocks[c] for c in which]

    over(x, plan.far)
    over(r, plan.far)
    x_others, r_others = share(x), share(r)
    over(x, plan.near)
    for c in plan.near:
        r[c] = after(r[c], *x_others)
    over(r, plan.near)

    x_all, hidden, to_a, to_b = forward(
        "forward_own_and_far", where, 0, pick(x, [0]), pick(x, plan.far), x_others, w_gate, w_up
    )
    r_all, grad_a, grad_b = backward(
        "backward_own_and_far", where, 0, pick(r, [0]), pick(r, plan.far), r_others, w_down, to_a, to_b
    )
    own, give, keep = first_grad(plan, where, grad_a, grad_b, w_gate, w_up, dp, cap)
    got = swap(give, "dp", 1)

    x_all, hidden, to_a, to_b = forward(
        "forward_near", where, 1, pick(x, plan.near), [], [], w_gate, w_up, (after(x_all, give), hidden)
    )
    far_sum = (keep + after(got, hidden).astype(F32)).astype(BF16)
    rows = 2 * cap
    far = [swap(far_sum[i * rows : (i + 1) * rows], "expert", 2 * c) for i, c in enumerate(plan.far)]
    kept = (after(r_all, far_sum), after(grad_a, give), after(grad_b, give))
    r_all, grad_a, grad_b = backward(
        "backward_near", where, 1, pick(r, plan.near), [], [], w_down, to_a, to_b, kept
    )
    away_part = near_grad(plan, where, grad_a, grad_b, w_gate, w_up, dp, cap, True)
    grad_a = after(grad_a, away_part[0], *far)
    here_part = near_grad(plan, where, grad_a, grad_b, w_gate, w_up, dp, cap, False)

    def send_back(part):
        return [swap(b, "expert", 2 * c) for b, c in zip(part, plan.near, strict=True)]

    away_rows, here_rows = send_back(away_part), send_back(here_part)
    slab = width // dp
    away, here = list(range(dp // 2, dp)), list(range(dp // 2))

    rights = [grad_a, grad_b]
    grads = outer("gate_and_up_0", where, after(x_all, here_part[0]), rights, 0, 4)
    away_rows[0] = after(away_rows[0], grads[0])
    away_sum, other = combine(
        plan, where, placings, [own, *far, *away_rows], dp, cap, away, True
    )
    other = swap(other, "expert", 1)
    away_sum = (away_sum + other.astype(F32)).astype(BF16)
    parts = [away_sum[:, n * slab : (n + 1) * slab] for n in range(len(away))]
    away_sums = [swap(part, "dp", s) for part, s in zip(parts, away, strict=True)]
    (grad_down,) = outer("down_grad", where, after(hidden, *parts), [r_all])
    here_rows[0] = after(here_rows[0], grad_down)
    total, other, *rest = combine(
        plan, where, placings, [own, *far, *here_rows], dp, cap, here, False
    )
    got = [swap(other, "expert", 1)]
    x_all = after(x_all, total)
    for part in range(1, 4):
        grads = outer(f"gate_and_up_{part}", where, x_all, rights, part, 4, grads)
        for n, s in enumerate(here[1:] if part == 1 else []):
            other = after(swap(rest[2 * n + 1], "expert", 1), grads[0])
            both = rest[2 * n].astype(F32) + other.astype(F32)
            got += [swap(both.astype(BF16), "dp", s)]
    grad_gate, grad_up = grads
    total = total + add_up(away_sums)
    for part in got:
        total = total + part.astype(F32)
    return (total.astype(BF16), grad_gate, grad_up, grad_down)


def solution(mesh):
    in_specs = (
        P("expert", None),
        P("expert", None),
        P("expert", None),
        P("expert", None),
        P("expert", None, "dp"),
        P("expert", None, "dp"),
        P("expert", "dp", None),
    )
    out_specs = (
        P("expert", "dp"),
        P("expert", None, "dp"),
        P("expert", None, "dp"),
        P("expert", "dp", None),
    )
    return jax.shard_map(body, mesh=mesh, in_specs=in_specs, out_specs=out_specs, check_vma=False)
```
